32 devices in a mesh: tile: 8 (over y, x, core), node: 4 (over z).
Axes of the slice: x: 2, y: 2, z: 4, core: 2. Of those that a mesh axis runs over, the one named last changes fastest.
Arguments:
- mask_field: float32 [512, 1024], P(None, 'tile'), may hold values from -1 to 1
- kernel_taps: float32 [4, 8, 2, 48, 65], P('node'), may hold values from -0.5 to 0.5
- kernel_weights: float32 [4, 8], P('node'), may hold values from 0.02 to 0.2
- node_weights: float32 [4], replicated, may hold values from 0.125 to 0.5
- node_index: int32 [4, 2], replicated, may hold values from 0 to 4
- freq_index: int32 [48], replicated, may hold values from -256 to 255, as said below
- chaos_weights: float32 [15], replicated, may hold values from 1 to 4
- target: bfloat16 [15, 512, 1024], P(None, None, 'tile'), may hold values from -3 to 3
Outputs:
- mask_gradient: float32 [512, 1024], P('node', 'tile')
The draws below stay inside these ranges and needn't reach their ends.
Inputs may be any that keep to these rules, and one draw needn't show every extreme that they name: `freq_index`: 48 distinct frequencies.
All inputs are finite; a program needn't handle non-finite values.
Results may differ from the reference program's by a relative error of at most 0.00085.
Values may be sent and summed in bfloat16 or wider, within the bound.
A program may use at most 64 MiB of HBM per device.

```python
import math
import jax
import jax.numpy as jnp
from jax import lax

Y = 512
NF = 48
K = 8
TAPS = 65
NCH = 15
LEVELS = 5
NODES = 4
COLS = 1024


def draw_freq_index(key, part):
    order = jax.random.permutation(key, Y)
    return (order[:NF] - Y // 2).astype(jnp.int32)


def touch_ends(drawn, own_key, smallest, top_value):
    longest = drawn.shape.index(max(drawn.shape))
    spots = []
    for shift in (0, 1):
        where = [jax.random.randint(jax.random.fold_in(own_key, axis), (), 0, length) for axis, length in enumerate(drawn.shape)]
        where[longest] = (where[longest] + shift) % drawn.shape[longest]
        spots.append(tuple(where))
    return drawn.at[spots[0]].set(smallest).at[spots[1]].set(top_value)


def level_of(key, extent, split, least, top_value):
    factor_of, own = 1.0, jax.random.fold_in(key, 6)
    for position, parts in split:
        draws = jnp.exp(jax.random.uniform(jax.random.fold_in(own, position), (parts,), jnp.float32, least / len(split), top_value / len(split)))
        factor_of = factor_of * jnp.repeat(draws, extent[position] // parts).reshape([-1 if axis == position else 1 for axis in range(len(extent))])
    return factor_of


def gaussian(key, shape, deviation, bound, cuts=(), kind=jnp.bfloat16):
    loudness = level_of(key, shape, cuts, -0.22, 0.18) if cuts else 1.0
    entries = jax.random.normal(key, shape, jnp.float32) * deviation * loudness
    return jnp.minimum(jnp.maximum(entries, -bound), bound).astype(kind)


def setup_inputs(seed: int = 0) -> dict:
    splits = jax.random.split(jax.random.key(seed), 9)
    mask_field = jnp.clip(jax.random.uniform(splits[0], (Y, COLS), jnp.float32, -1.0, 1.0) * level_of(splits[0], (Y, COLS), ((1, 8),), -0.4, 0.0), -1.0, 1.0)
    kernel_taps = gaussian(splits[1], (NODES, K, 2, NF, TAPS), (2 * TAPS) ** -0.5, 0.5, ((0, 4),), jnp.float32)
    kernel_weights = jnp.clip(jnp.exp(math.log(0.2) - 2.3025851 * jax.random.uniform(splits[2], (NODES, K), jnp.float32) ** level_of(splits[2], (NODES, K), ((0, 4),), -0.2, 0.2)), 0.02, 0.2)
    node_weights = jnp.clip(jnp.exp(jax.random.uniform(splits[3], (NODES,), jnp.float32, math.log(0.125), math.log(0.5))), 0.125, 0.5)
    node_index = touch_ends(jax.random.randint(splits[4], (NODES, 2), 0, LEVELS), jax.random.fold_in(splits[4], 1), 0, LEVELS - 1).astype(jnp.int32)
    freq_index = draw_freq_index(jax.random.fold_in(splits[8], 71), 0)
    chaos_weights = jnp.clip(jnp.exp(jax.random.uniform(splits[6], (NCH,), jnp.float32, math.log(1.0), math.log(4.0))), 1.0, 4.0)
    target = gaussian(splits[7], (NCH, Y, COLS), 0.5, 3.0, ((2, 8),))
    return {"mask_field": mask_field, "kernel_taps": kernel_taps, "kernel_weights": kernel_weights, "node_weights": node_weights, "node_index": node_index, "freq_index": freq_index, "chaos_weights": chaos_weights, "target": target}


highest = lax.Precision.HIGHEST
resist_slope = 4.0
resist_level = 0.6

def spectra_tables(freq_index, pixel_rows):
    row_line = jnp.arange(pixel_rows, dtype=jnp.int32)
    phase_angle = jnp.mod(freq_index[:, None] * row_line[None, :], pixel_rows).astype(jnp.float32) * (2.0 * math.pi / pixel_rows)
    cosine_table = jnp.cos(phase_angle)
    sine_table = jnp.sin(phase_angle)
    forward = jnp.concatenate([cosine_table, -sine_table], 0) / math.sqrt(pixel_rows)
    freq_count = freq_index.shape[0]
    upper = jnp.concatenate([cosine_table.T, -sine_table.T], 1)
    lower = jnp.concatenate([sine_table.T, cosine_table.T], 1)
    inverse = jnp.concatenate([upper, lower], 0) / math.sqrt(freq_count)
    return (forward, inverse)

def legendre_set(coordinate):
    square = coordinate * coordinate
    return [jnp.ones_like(coordinate), coordinate, 1.5 * square - 0.5, (2.5 * square - 1.5) * coordinate, (4.375 * square - 3.75) * square + 0.375]

def level_coords(node_index):
    return node_index.astype(jnp.float32) * (2.0 / (LEVELS - 1)) - 1.0

def chaos_basis(node_index):
    coords = level_coords(node_index)
    focus_poly = legendre_set(coords[:, 0])
    dose_poly = legendre_set(coords[:, 1])
    columns = []
    for degree in range(5):
        for focus_order in range(degree, -1, -1):
            columns.append(focus_poly[focus_order] * dose_poly[degree - focus_order])
    return jnp.stack(columns, 1)

def dose_levels(node_index):
    return 1.0 + 0.1 * level_coords(node_index)[:, 1]

def resist_image(spectrum, taps_node, weights_node, dose_scale, inverse, col_count, radius):
    freq_count = taps_node.shape[2]
    shifted = jnp.stack([spectrum[:, offset:offset + col_count] for offset in range(2 * radius + 1)], 1)
    real_part = shifted[:freq_count]
    imag_part = shifted[freq_count:]
    taps_real = taps_node[:, 0]
    taps_imag = taps_node[:, 1]
    band_real = jnp.einsum('fsx,kfs->kfx', real_part, taps_real, precision=highest) - jnp.einsum('fsx,kfs->kfx', imag_part, taps_imag, precision=highest)
    band_imag = jnp.einsum('fsx,kfs->kfx', real_part, taps_imag, precision=highest) + jnp.einsum('fsx,kfs->kfx', imag_part, taps_real, precision=highest)
    stacked = jnp.concatenate([band_real, band_imag], 1)
    fields = jnp.einsum('yf,kfx->kyx', inverse, stacked, precision=highest)
    pixel_rows = inverse.shape[0] // 2
    powers = fields[:, :pixel_rows] * fields[:, :pixel_rows] + fields[:, pixel_rows:] * fields[:, pixel_rows:]
    intensity = jnp.einsum('k,kyx->yx', weights_node, powers, precision=highest)
    return jax.nn.sigmoid(resist_slope * (dose_scale * intensity - resist_level))

def reference(mask_field, kernel_taps, kernel_weights, node_weights, node_index, freq_index, chaos_weights, target):
    pixel_rows, col_count = mask_field.shape
    radius = (kernel_taps.shape[-1] - 1) // 2
    forward, inverse = spectra_tables(freq_index, pixel_rows)
    padded = jnp.pad(mask_field, ((0, 0), (radius, radius)))
    spectrum = jnp.dot(forward, padded, precision=highest)
    node_basis = chaos_basis(node_index)
    dose_scale = dose_levels(node_index)
    node_count = node_weights.shape[0]
    node_line = jnp.arange(node_count, dtype=jnp.int32)

    def image_of(spec, node_pos):
        return resist_image(spec, kernel_taps[node_pos], kernel_weights[node_pos], dose_scale[node_pos], inverse, col_count, radius)

    def add_node(running, node_pos):
        rounded = lax.optimization_barrier(image_of(spectrum, node_pos).astype(jnp.bfloat16))
        scaled = node_weights[node_pos] * node_basis[node_pos]
        return (running + scaled[:, None, None] * rounded.astype(jnp.float32)[None], None)
    coefficient, _ = lax.scan(add_node, jnp.zeros((node_basis.shape[1], pixel_rows, col_count), jnp.float32), node_line)
    mixed_terms = chaos_weights[:, None, None] * jnp.tanh(coefficient - target.astype(jnp.float32))

    def add_grad(running, node_pos):
        pressure = node_weights[node_pos] * jnp.einsum('j,jyx->yx', node_basis[node_pos], mixed_terms, precision=highest)
        resist, pullback = jax.vjp(lambda spec: image_of(spec, node_pos), spectrum)
        dspec, = pullback(pressure)
        return (running + dspec, None)
    dspec_sum, _ = lax.scan(add_grad, jnp.zeros_like(spectrum), node_line)
    grad_padded = jnp.dot(forward.T, dspec_sum, precision=highest)
    return grad_padded[:, radius:radius + col_count]
```

```python
import functools
import math

import jax
import jax.numpy as jnp
import ml_dtypes
import numpy as np
from jax import lax
from jax.experimental import pallas as pl
from jax.experimental.pallas import tpu as pltpu
from jax.sharding import PartitionSpec as P

LEVELS = 5
DEGREES = 5
MESH = pl.DeviceIdType.MESH
bf16 = jnp.bfloat16
f32 = jnp.float32
resist_slope = 4.0
resist_level = 0.6


def split(value):
    high = value.astype(bf16)
    return high, (value - high.astype(f32)).astype(bf16)


def mm(left, right):
    return jnp.dot(left, right, preferred_element_type=f32)


def mm3(left, right):
    return mm(left[0], right[0]) + (mm(left[0], right[1]) + mm(left[1], right[0]))


def half_turn_cosine(step, half):
    folded = jnp.abs((step & (2 * half - 1)) - half).astype(f32)
    t = folded * (2.0 / half) - 1.0
    s = t * t
    acc = jnp.full_like(t, 5.6921729e-8)
    for c in (-3.5988432e-6, 1.6044118e-4, -4.6817541e-3, 7.9692626e-2, -0.64596410, 1.57079633):
        acc = acc * s + c
    return acc * t


def legendre(u):
    s = u * u
    return [None, u, 1.5 * s - 0.5, (2.5 * s - 1.5) * u, (4.375 * s - 3.75) * s + 0.375]


def level(index):
    return index.astype(f32) * (2.0 / (LEVELS - 1)) - 1.0


def basis_of(node_index, node):
    focus = legendre(level(node_index[node, 0]))
    dose = legendre(level(node_index[node, 1]))
    terms = []
    for degree in range(DEGREES):
        for p in range(degree, -1, -1):
            a, b = focus[p], dose[degree - p]
            terms.append(1.0 if a is None and b is None else b if a is None else a if b is None else a * b)
    return terms


def column_tables(cols, radius, freq_count):
    ring = 2 * cols
    w = np.arange(ring)
    angle = 2 * np.pi * ((w[:, None] * w[None, :]) % ring) / ring
    direct = np.concatenate([np.cos(angle), np.sin(angle)], 1)
    out = 2 * np.pi * ((w[:, None] * (np.arange(cols) + cols - radius)[None, :]) % ring) / ring
    c, s = np.cos(out), np.sin(out)
    back = np.concatenate([np.concatenate([c, s], 1), np.concatenate([-s, c], 1)], 0)
    back = back / (ring * math.sqrt(freq_count))
    pieces = []
    for table in (direct, back, back.T):
        high = table.astype(ml_dtypes.bfloat16)
        low = (table - high.astype(np.float64)).astype(ml_dtypes.bfloat16)
        pieces.append(np.stack([high, low]))
    return pieces


def kernel(
    tiles, nodes, radius,
    mask, taps, kernel_weights, node_weights, node_index, freq, chaos_weights, target,
    direct, back, back_t,
    out,
    freq_rows, freq_lanes, cos_in, sin_in, trans, own_table, padded_taps, gains,
    own_spec, halo, stacked, cos_part, sin_part, resist, own_image, images, term, term_rev,
    push, pressure, dfield, dparts, zin, ein, total, gathered,
    local_sem, halo_send, halo_recv, image_send, image_recv, push_send, push_recv,
    z_send, z_recv, e_send, e_recv, g_send, g_recv,
):
    tile, node = lax.axis_index("tile"), lax.axis_index("node")
    right, left = lax.rem(tile + 1, tiles), lax.rem(tile + tiles - 1, tiles)
    rows, cols = mask.shape
    half = rows // 2
    chunk = half // nodes
    freq_count = freq.shape[0]
    terms = chaos_weights.shape[0]
    kernels = taps.shape[0] // 2
    share = 2 * freq_count // nodes

    def after(d):
        return lax.rem(node + d, nodes)

    def before(d):
        return lax.rem(node + nodes - d, nodes)

    barrier = pltpu.get_barrier_semaphore()
    for d in range(1, nodes):
        pl.semaphore_signal(barrier, inc=1, device_id=(tile, after(d)), device_id_type=MESH)
    for d in range(nodes):
        pl.semaphore_signal(barrier, inc=1, device_id=(right, after(d)), device_id_type=MESH)
        pl.semaphore_signal(barrier, inc=1, device_id=(left, after(d)), device_id_type=MESH)

    upper = pltpu.make_async_copy(
        target.at[:, pl.ds(pl.multiple_of(node * chunk, chunk), chunk), :], term.at[0], local_sem.at[0]
    )
    lower = pltpu.make_async_copy(
        target.at[:, pl.ds(pl.multiple_of(rows - (node + 1) * chunk, chunk), chunk), :],
        term.at[1], local_sem.at[1],
    )
    upper.start()
    lower.start()

    row_id = lax.broadcasted_iota(jnp.int32, freq_rows.shape, 0)
    lane_id = lax.broadcasted_iota(jnp.int32, freq_lanes.shape, 1) % freq_count
    by_row = jnp.zeros(freq_rows.shape, jnp.int32)
    by_lane = jnp.zeros(freq_lanes.shape, jnp.int32)
    for i in range(freq_count):
        by_row = jnp.where(row_id == i, freq[i], by_row)
        by_lane = jnp.where(lane_id == i, freq[i], by_lane)
    freq_rows[...] = by_row
    freq_lanes[...] = by_lane

    place = lax.broadcasted_iota(jnp.int32, (freq_count, half), 1)
    step = freq_rows[:, :1] * (2 * place + 1)
    c_high, c_low = split(half_turn_cosine(step, rows))
    s_high, s_low = split(half_turn_cosine(step - half, rows))
    trans[0, :, :half] = c_high
    trans[1, :, :half] = c_low
    trans[0, :, half:] = s_high
    trans[1, :, half:] = s_low

    ri = lax.broadcasted_iota(jnp.int32, (half, half), 0)
    ci = lax.broadcasted_iota(jnp.int32, (half, half), 1)
    mirror = jnp.where(ri + ci == half - 1, 1.0, 0.0).astype(bf16)
    m_high, m_low = split(mask[half:, :])
    mirrored = mm(mirror, m_high) + mm(mirror, m_low)
    top = mask[:half, :]
    norm = 1.0 / math.sqrt(rows)
    own_spec[:freq_count, :] = mm3((c_high, c_low), split(top + mirrored)) * norm
    own_spec[freq_count:, :] = mm3((s_high, s_low), split(top - mirrored)) * -norm

    pl.semaphore_wait(barrier, 3 * nodes - 1)
    halo_copies = []
    for side, to in ((0, right), (1, left)):
        halo_copies.append(pltpu.make_async_remote_copy(
            src_ref=own_spec, dst_ref=halo.at[side], send_sem=halo_send.at[side],
            recv_sem=halo_recv.at[side], device_id=(to, node), device_id_type=MESH,
        ))
        halo_copies[-1].start()

    wide = 3 * freq_count
    place = lax.broadcasted_iota(jnp.int32, (half, wide), 0)
    lane = lax.broadcasted_iota(jnp.int32, (half, wide), 1)
    middle = (lane >= freq_count) & (lane < 2 * freq_count)
    step = freq_lanes[:1, :wide] * (2 * place + 1)
    for table, value in ((cos_in, half_turn_cosine(step, rows)), (sin_in, half_turn_cosine(step - half, rows))):
        rounded = value.astype(bf16).astype(f32)
        table[...] = jnp.where(middle, value - rounded, rounded).astype(bf16)

    own_rows = rows // nodes
    place = lax.broadcasted_iota(jnp.int32, (own_rows, 2 * freq_count), 0) + node * own_rows
    lane = lax.broadcasted_iota(jnp.int32, (own_rows, 2 * freq_count), 1)
    step = freq_lanes[:1, : 2 * freq_count] * (2 * place + 1)
    step = jnp.where(lane < freq_count, step, step + half)
    own_table[0], own_table[1] = split(half_turn_cosine(step, rows) * norm)

    padded_taps[...] = jnp.zeros(padded_taps.shape, f32)
    for i in range(2 * kernels):
        padded_taps[i * freq_count : (i + 1) * freq_count, : 2 * radius + 1] = taps[i]
    near = padded_taps.shape[1]
    t = mm3(split(padded_taps[...]), (direct[0, :near, :], direct[1, :near, :]))
    ring = 2 * cols
    for k in range(kernels):
        re = t[2 * k * freq_count : (2 * k + 1) * freq_count]
        im = t[(2 * k + 1) * freq_count : (2 * k + 2) * freq_count]
        gains[k, :, :ring] = re[:, :ring] - im[:, ring:]
        gains[k, :, ring:] = re[:, ring:] + im[:, :ring]

    ri = lax.broadcasted_iota(jnp.int32, (chunk, chunk), 0)
    ci = lax.broadcasted_iota(jnp.int32, (chunk, chunk), 1)
    small_mirror = jnp.where(ri + ci == chunk - 1, 1.0, 0.0).astype(bf16)
    upper.wait()
    lower.wait()
    for j in range(terms):
        term_rev[j] = mm(small_mirror, term[1, j]).astype(bf16)

    for copy in halo_copies:
        copy.wait()
    lane = lax.broadcasted_iota(jnp.int32, (2 * freq_count, cols), 1)
    keep_left = jnp.where((lane >= cols - radius) & (tile > 0), 1.0, 0.0)
    keep_right = jnp.where((lane < radius) & (tile < tiles - 1), 1.0, 0.0)
    around = jnp.concatenate([halo[0] * keep_left + halo[1] * keep_right, own_spec[...]], 1)
    t = mm3(split(around), (direct[0], direct[1]))
    a_re = t[:freq_count, :ring] + t[freq_count:, ring:]
    a_im = t[freq_count:, :ring] - t[:freq_count, ring:]
    products = []
    for k in range(kernels):
        g_re, g_im = gains[k, :, :ring], gains[k, :, ring:]
        products.append(jnp.concatenate([a_re * g_re - a_im * g_im, a_re * g_im + a_im * g_re], 1))
    band = mm3(split(jnp.concatenate(products, 0)), (back[0], back[1]))
    for k in range(kernels):
        high, low = split(band[k * freq_count : (k + 1) * freq_count])
        for part in range(2):
            at = (part * kernels + k) * cols
            source = slice(part * cols, (part + 1) * cols)
            stacked[:freq_count, at : at + cols] = high[:, source]
            stacked[freq_count : 2 * freq_count, at : at + cols] = high[:, source]
            stacked[2 * freq_count :, at : at + cols] = low[:, source]

    def image_copy(d):
        return pltpu.make_async_remote_copy(
            src_ref=own_image.at[after(d)], dst_ref=images.at[d], send_sem=image_send.at[d],
            recv_sem=image_recv.at[d], device_id=(tile, after(d)), device_id_type=MESH,
        )

    dose = 1.0 + 0.1 * level(node_index[node, 1])
    side = kernels * cols

    def fields(row, count, k):
        p = cos_part[pl.ds(row, count), k * cols : (k + 1) * cols]
        t = cos_part[pl.ds(row, count), side + k * cols : side + (k + 1) * cols]
        r = sin_part[pl.ds(row, count), k * cols : (k + 1) * cols]
        q = sin_part[pl.ds(row, count), side + k * cols : side + (k + 1) * cols]
        return p - q, r + t, p + q, t - r

    piece = min(32, chunk)
    for d in list(range(1, nodes)) + [0]:
        mine = after(d)
        row = pl.multiple_of(mine * chunk, chunk)
        cos_part[pl.ds(row, chunk), :] = mm(cos_in[pl.ds(row, chunk), :], stacked[...])
        sin_part[pl.ds(row, chunk), :] = mm(sin_in[pl.ds(row, chunk), :], stacked[...])

        for part in range(chunk // piece):
            at = pl.multiple_of(row + part * piece, piece)
            first = jnp.zeros((piece, cols), f32)
            second = jnp.zeros((piece, cols), f32)
            for k in range(kernels):
                a, b, c, e = fields(at, piece, k)
                weight = kernel_weights[0, k]
                first = first + weight * (a * a + b * b)
                second = second + weight * (c * c + e * e)
            for h, intensity in ((0, first), (1, second)):
                value = jax.nn.sigmoid(resist_slope * (dose * intensity - resist_level))
                resist[h, pl.ds(at, piece), :] = value
                if d:
                    own_image[mine, h, part * piece : (part + 1) * piece, :] = value.astype(bf16)
                else:
                    images[0, h, part * piece : (part + 1) * piece, :] = value.astype(bf16)
        if d:
            image_copy(d).start()

    sources = [before(d) for d in range(nodes)]
    bases = [basis_of(node_index, n) for n in sources]
    weights = [node_weights[n] for n in sources]
    scaled = [[weights[d] * b for b in bases[d]] for d in range(nodes)]
    for d in range(1, nodes):
        image_copy(d).wait()
    for h in range(2):
        for part in range(chunk // piece):
            at = slice(part * piece, (part + 1) * piece)
            seen = [images[d, h, at, :].astype(f32) for d in range(nodes)]
            sums = [None] * nodes
            for j in range(terms):
                coefficient = scaled[0][j] * seen[0]
                for d in range(1, nodes):
                    coefficient = coefficient + scaled[d][j] * seen[d]
                wanted = term[0, j, at, :] if h == 0 else term_rev[j, at, :]
                mixed = chaos_weights[j] * jnp.tanh(coefficient - wanted.astype(f32))
                for d in range(nodes):
                    one = scaled[d][j] * mixed
                    sums[d] = one if sums[d] is None else sums[d] + one
            for d in range(nodes):
                if d:
                    push[d, h, at, :] = sums[d]
                else:
                    pressure[0, h, at, :] = sums[d]

    def push_copy(d):
        return pltpu.make_async_remote_copy(
            src_ref=push.at[d], dst_ref=pressure.at[d], send_sem=push_send.at[d],
            recv_sem=push_recv.at[d], device_id=(tile, before(d)), device_id_type=MESH,
        )

    for d in range(1, nodes):
        push_copy(d).start()

    for d in range(nodes):
        if d:
            push_copy(d).wait()
        row = pl.multiple_of(after(d) * chunk, chunk)
        for part in range(chunk // piece):
            at = pl.multiple_of(row + part * piece, piece)
            slopes = []
            for h in range(2):
                value = resist[h, pl.ds(at, piece), :]
                given = pressure[d, h, part * piece : (part + 1) * piece, :]
                slopes.append(given * value * (1.0 - value) * (resist_slope * dose))
            for k in range(kernels):
                a, b, c, e = fields(at, piece, k)
                a, b, c, e = a * slopes[0], b * slopes[0], c * slopes[1], e * slopes[1]
                for base, where, value in ((0, 0, a + c), (0, side, b + e), (half, 0, b - e), (half, side, c - a)):
                    high, low = split(value)
                    lanes = slice(where + k * cols, where + (k + 1) * cols)
                    dfield[0, pl.ds(base + at, piece), lanes] = high
                    dfield[1, pl.ds(base + at, piece), lanes] = low
    both = trans[...].reshape(2 * freq_count, 2 * half)
    t = mm(both, dfield[0])
    dband = t[:freq_count] + t[freq_count:] + mm(trans[0], dfield[1])
    pieces = []
    for k in range(kernels):
        one = jnp.concatenate([dband[:, k * cols : (k + 1) * cols], dband[:, side + k * cols : side + (k + 1) * cols]], 1)
        pieces.append(one * (2.0 * kernel_weights[0, k]))
    t = mm3(split(jnp.concatenate(pieces, 0)), (back_t[0], back_t[1]))
    z_re = jnp.zeros((freq_count, ring), f32)
    z_im = jnp.zeros((freq_count, ring), f32)
    for k in range(kernels):
        d_re = t[k * freq_count : (k + 1) * freq_count, :ring]
        d_im = t[k * freq_count : (k + 1) * freq_count, ring:]
        g_re, g_im = gains[k, :, :ring], gains[k, :, ring:]
        z_re = z_re + (g_re * d_re + g_im * d_im)
        z_im = z_im + (g_re * d_im - g_im * d_re)
    t = mm3(split(jnp.concatenate([z_re, z_im], 0)), (direct[0], direct[1]))
    dspec = jnp.concatenate(
        [t[:freq_count, :ring] - t[freq_count:, ring:], t[:freq_count, ring:] + t[freq_count:, :ring]], 0
    )
    for n in range(nodes):
        for block in range(2):
            dparts[n, block] = dspec[n * share : (n + 1) * share, block * cols : (block + 1) * cols]

    def z_copy(d):
        return pltpu.make_async_remote_copy(
            src_ref=dparts.at[after(d), 1], dst_ref=zin.at[d], send_sem=z_send.at[d],
            recv_sem=z_recv.at[d], device_id=(tile, after(d)), device_id_type=MESH,
        )

    def e_copy(d, side_id):
        to = right if side_id == 0 else left
        return pltpu.make_async_remote_copy(
            src_ref=dparts.at[after(d), 0], dst_ref=ein.at[side_id, d], send_sem=e_send.at[side_id, d],
            recv_sem=e_recv.at[side_id, d], device_id=(to, after(d)), device_id_type=MESH,
        )

    copies = []
    for d in range(nodes):
        copies += [e_copy(d, 0), e_copy(d, 1)]
        if d:
            copies.append(z_copy(d))
    for copy in copies:
        copy.start()
    for copy in copies:
        copy.wait()
    lane = lax.broadcasted_iota(jnp.int32, (share, cols), 1)
    keep_left = jnp.where((lane < radius) & (tile > 0), 1.0, 0.0)
    keep_right = jnp.where((lane >= cols - radius) & (tile < tiles - 1), 1.0, 0.0)
    value = dparts[node, 1]
    for d in range(nodes):
        if d:
            value = value + zin[d]
        value = value + ein[0, d] * keep_left + ein[1, d] * keep_right
    total[...] = value
    gathered[node] = value

    def g_copy(d):
        return pltpu.make_async_remote_copy(
            src_ref=total, dst_ref=gathered.at[node], send_sem=g_send.at[d],
            recv_sem=g_recv.at[d], device_id=(tile, after(d)), device_id_type=MESH,
        )

    for d in range(1, nodes):
        g_copy(d).start()
    for d in range(1, nodes):
        g_copy(d).wait()
    summed = jnp.concatenate([gathered[n] for n in range(nodes)], 0)
    out[...] = mm3((own_table[0], own_table[1]), split(summed))


def local(
    tiles, nodes,
    mask_field, kernel_taps, kernel_weights, node_weights, node_index, freq_index, chaos_weights, target,
):
    rows, cols = mask_field.shape
    _, kernels, _, freq_count, tap_count = kernel_taps.shape
    radius = (tap_count - 1) // 2
    half, chunk = rows // 2, rows // 2 // nodes
    terms = chaos_weights.shape[0]
    ring = 2 * cols
    share = 2 * freq_count // nodes
    direct, back, back_t = column_tables(cols, radius, freq_count)
    vmem = pl.BlockSpec(memory_space=pltpu.VMEM)
    smem = pl.BlockSpec(memory_space=pltpu.SMEM)
    scratch = pltpu.VMEM
    dma = pltpu.SemaphoreType.DMA
    return pl.pallas_call(
        functools.partial(kernel, tiles, nodes, radius),
        out_shape=jax.ShapeDtypeStruct((rows // nodes, cols), f32),
        in_specs=[vmem, vmem, smem, smem, smem, smem, smem, pl.BlockSpec(memory_space=pl.ANY), vmem, vmem, vmem],
        out_specs=vmem,
        scratch_shapes=[
            scratch((freq_count, 128), jnp.int32),
            scratch((8, 256), jnp.int32),
            scratch((half, 3 * freq_count), bf16),
            scratch((half, 3 * freq_count), bf16),
            scratch((2, freq_count, 2 * half), bf16),
            scratch((2, rows // nodes, 2 * freq_count), bf16),
            scratch((2 * kernels * freq_count, 128), f32),
            scratch((kernels, freq_count, 2 * ring), f32),
            scratch((2 * freq_count, cols), f32),
            scratch((2, 2 * freq_count, cols), f32),
            scratch((3 * freq_count, 2 * kernels * cols), bf16),
            scratch((half, 2 * kernels * cols), f32),
            scratch((half, 2 * kernels * cols), f32),
            scratch((2, half, cols), f32),
            scratch((nodes, 2, chunk, cols), bf16),
            scratch((nodes, 2, chunk, cols), bf16),
            scratch((2, terms, chunk, cols), bf16),
            scratch((terms, chunk, cols), bf16),
            scratch((nodes, 2, chunk, cols), f32),
            scratch((nodes, 2, chunk, cols), f32),
            scratch((2, 2 * half, 2 * kernels * cols), bf16),
            scratch((nodes, 2, share, cols), f32),
            scratch((nodes, share, cols), f32),
            scratch((2, nodes, share, cols), f32),
            scratch((share, cols), f32),
            scratch((nodes, share, cols), f32),
            dma((2,)), dma((2,)), dma((2,)),
            dma((nodes,)), dma((nodes,)), dma((nodes,)), dma((nodes,)),
            dma((nodes,)), dma((nodes,)), dma((2, nodes)), dma((2, nodes)),
            dma((nodes,)), dma((nodes,)),
        ],
        compiler_params=pltpu.CompilerParams(
            collective_id=0, has_side_effects=True, vmem_limit_bytes=48 * 1024 * 1024
        ),
        name="mask_gradient",
    )(
        mask_field, kernel_taps.reshape(2 * kernels, freq_count, tap_count), kernel_weights, node_weights,
        node_index, freq_index, chaos_weights, target, direct, back, back_t,
    )


def solution(mesh):
    placed = (
        P(None, "tile"),
        P("node", None, None, None, None),
        P("node", None),
        P(),
        P(),
        P(),
        P(),
        P(None, None, "tile"),
    )
    return jax.shard_map(
        functools.partial(local, mesh.shape["tile"], mesh.shape["node"]),
        mesh=mesh, in_specs=placed, out_specs=P("node", "tile"), check_vma=False,
    )
```

```python
import functools
import math

import jax
import jax.numpy as jnp
import ml_dtypes
import numpy as np
from jax import lax
from jax.experimental import pallas as pl
from jax.experimental.pallas import tpu as pltpu
from jax.sharding import PartitionSpec as P

LEVELS = 5
DEGREES = 5
MESH = pl.DeviceIdType.MESH
bf16 = jnp.bfloat16
f32 = jnp.float32
resist_slope = 4.0
resist_level = 0.6


def split(value):
    high = value.astype(bf16)
    return high, (value - high.astype(f32)).astype(bf16)


def mm(left, right):
    return jnp.dot(left, right, preferred_element_type=f32)


def mm3(left, right):
    count = left[0].shape[0]
    both = mm(jnp.concatenate(left, 0), right[0])
    return both[:count] + (mm(left[0], right[1]) + both[count:])


def half_turn_cosine(step, half):
    folded = jnp.abs((step & (2 * half - 1)) - half).astype(f32)
    t = folded * (2.0 / half) - 1.0
    s = t * t
    acc = jnp.full_like(t, 5.6921729e-8)
    for c in (-3.5988432e-6, 1.6044118e-4, -4.6817541e-3, 7.9692626e-2, -0.64596410, 1.57079633):
        acc = acc * s + c
    return acc * t


def legendre(u):
    s = u * u
    return [None, u, 1.5 * s - 0.5, (2.5 * s - 1.5) * u, (4.375 * s - 3.75) * s + 0.375]


def level(index):
    return index.astype(f32) * (2.0 / (LEVELS - 1)) - 1.0


def basis_of(node_index, node):
    focus = legendre(level(node_index[0, node]))
    dose = legendre(level(node_index[1, node]))
    terms = []
    for degree in range(DEGREES):
        for p in range(degree, -1, -1):
            a, b = focus[p], dose[degree - p]
            terms.append(1.0 if a is None and b is None else b if a is None else a if b is None else a * b)
    return terms


def column_tables(cols, radius, freq_count):
    ring = 2 * cols
    w = np.arange(ring)
    angle = 2 * np.pi * ((w[:, None] * w[None, :]) % ring) / ring
    direct = np.concatenate([np.cos(angle), np.sin(angle)], 1)
    out = 2 * np.pi * ((w[:, None] * (np.arange(cols) + cols - radius)[None, :]) % ring) / ring
    c, s = np.cos(out), np.sin(out)
    back = np.concatenate([np.concatenate([c, s], 1), np.concatenate([-s, c], 1)], 0)
    back = back / (ring * math.sqrt(freq_count))
    pieces = []
    for table in (direct, back, back.T):
        high = table.astype(ml_dtypes.bfloat16)
        low = (table - high.astype(np.float64)).astype(ml_dtypes.bfloat16)
        pieces.append(np.stack([high, low]))
    return pieces


def kernel(
    tiles, nodes, radius,
    mask_hbm, taps_hbm, kernel_weights, node_weights, node_index, freq, chaos_weights, target,
    direct_hbm, back_hbm, back_t_hbm,
    out,
    mask, taps, direct, back, back_t,
    freq_rows, freq_lanes, cos_in, sin_in, trans, own_table, padded_taps, gains,
    own_spec, halo, stacked, cos_part, sin_part, resist, own_image, images, term,
    push, pressure, dfield, dparts, zin, ein, total, gathered,
    local_sem, halo_send, halo_recv, image_send, image_recv, push_send, push_recv,
    z_send, z_recv, e_send, e_recv, g_send, g_recv,
):
    tile, node = lax.axis_index("tile"), lax.axis_index("node")
    right, left = lax.rem(tile + 1, tiles), lax.rem(tile + tiles - 1, tiles)
    rows, cols = mask.shape
    half = rows // 2
    chunk = half // nodes
    freq_count = freq.shape[0]
    terms = chaos_weights.shape[0]
    kernels = taps.shape[0] // 2
    share = 2 * freq_count // nodes

    def after(d):
        return lax.rem(node + d, nodes)

    def before(d):
        return lax.rem(node + nodes - d, nodes)

    barrier = pltpu.get_barrier_semaphore()
    for d in range(1, nodes):
        pl.semaphore_signal(barrier, inc=1, device_id=(tile, after(d)), device_id_type=MESH)
    for d in range(nodes):
        pl.semaphore_signal(barrier, inc=1, device_id=(right, after(d)), device_id_type=MESH)
        pl.semaphore_signal(barrier, inc=1, device_id=(left, after(d)), device_id_type=MESH)

    loads = []
    for i, (source, held) in enumerate((
        (mask_hbm, mask), (direct_hbm, direct), (taps_hbm, taps), (back_hbm, back), (back_t_hbm, back_t),
    )):
        loads.append(pltpu.make_async_copy(source, held, local_sem.at[i + 2]))
    for load in loads[:3]:
        load.start()
    upper = pltpu.make_async_copy(
        target.at[:, pl.ds(pl.multiple_of(node * chunk, chunk), chunk), :], term.at[0], local_sem.at[0]
    )
    lower = pltpu.make_async_copy(
        target.at[:, pl.ds(pl.multiple_of(rows - (node + 1) * chunk, chunk), chunk), :],
        term.at[1], local_sem.at[1],
    )
    upper.start()
    lower.start()
    for load in loads[3:]:
        load.start()

    row_id = lax.broadcasted_iota(jnp.int32, freq_rows.shape, 0)
    lane_id = lax.broadcasted_iota(jnp.int32, freq_lanes.shape, 1) % freq_count
    by_row = jnp.zeros(freq_rows.shape, jnp.int32)
    by_lane = jnp.zeros(freq_lanes.shape, jnp.int32)
    for i in range(freq_count):
        by_row = jnp.where(row_id == i, freq[i], by_row)
        by_lane = jnp.where(lane_id == i, freq[i], by_lane)
    freq_rows[...] = by_row
    freq_lanes[...] = by_lane

    place = lax.broadcasted_iota(jnp.int32, (freq_count, half), 1)
    step = freq_rows[:, :1] * (2 * place + 1)
    c_high, c_low = split(half_turn_cosine(step, rows))
    s_high, s_low = split(half_turn_cosine(step - half, rows))
    trans[0, :, :half] = c_high
    trans[1, :, :half] = c_low
    trans[0, :, half:] = s_high
    trans[1, :, half:] = s_low

    ri = lax.broadcasted_iota(jnp.int32, (half, half), 0)
    ci = lax.broadcasted_iota(jnp.int32, (half, half), 1)
    mirror = jnp.where(ri + ci == half - 1, 1.0, 0.0).astype(bf16)
    loads[0].wait()
    m_high, m_low = split(mask[half:, :])
    mirrored = mm(mirror, m_high) + mm(mirror, m_low)
    top = mask[:half, :]
    norm = 1.0 / math.sqrt(rows)
    own_spec[:freq_count, :] = mm3((c_high, c_low), split(top + mirrored)) * norm
    own_spec[freq_count:, :] = mm3((s_high, s_low), split(top - mirrored)) * -norm

    pl.semaphore_wait(barrier, 3 * nodes - 1)
    halo_copies = []
    for side, to in ((0, right), (1, left)):
        halo_copies.append(pltpu.make_async_remote_copy(
            src_ref=own_spec, dst_ref=halo.at[side], send_sem=halo_send.at[side],
            recv_sem=halo_recv.at[side], device_id=(to, node), device_id_type=MESH,
        ))
        halo_copies[-1].start()

    wide = 3 * freq_count
    place = lax.broadcasted_iota(jnp.int32, (half, wide), 0)
    lane = lax.broadcasted_iota(jnp.int32, (half, wide), 1)
    middle = (lane >= freq_count) & (lane < 2 * freq_count)
    step = freq_lanes[:1, :wide] * (2 * place + 1)
    for table, value in ((cos_in, half_turn_cosine(step, rows)), (sin_in, half_turn_cosine(step - half, rows))):
        rounded = value.astype(bf16).astype(f32)
        table[...] = jnp.where(middle, value - rounded, rounded).astype(bf16)

    own_rows = rows // nodes
    place = lax.broadcasted_iota(jnp.int32, (own_rows, 2 * freq_count), 0) + node * own_rows
    lane = lax.broadcasted_iota(jnp.int32, (own_rows, 2 * freq_count), 1)
    step = freq_lanes[:1, : 2 * freq_count] * (2 * place + 1)
    step = jnp.where(lane < freq_count, step, step + half)
    own_table[0], own_table[1] = split(half_turn_cosine(step, rows) * norm)

    padded_taps[...] = jnp.zeros(padded_taps.shape, f32)
    loads[1].wait()
    loads[2].wait()
    for i in range(2 * kernels):
        padded_taps[i * freq_count : (i + 1) * freq_count, : 2 * radius + 1] = taps[i]
    near = padded_taps.shape[1]
    t = mm3(split(padded_taps[...]), (direct[0, :near, :], direct[1, :near, :]))
    ring = 2 * cols
    for k in range(kernels):
        re = t[2 * k * freq_count : (2 * k + 1) * freq_count]
        im = t[(2 * k + 1) * freq_count : (2 * k + 2) * freq_count]
        gains[k, :, :ring] = re[:, :ring] - im[:, ring:]
        gains[k, :, ring:] = re[:, ring:] + im[:, :ring]

    ri = lax.broadcasted_iota(jnp.int32, (chunk, chunk), 0)
    ci = lax.broadcasted_iota(jnp.int32, (chunk, chunk), 1)
    small_mirror = jnp.where(ri + ci == chunk - 1, 1.0, 0.0).astype(bf16)
    upper.wait()
    lower.wait()
    turned = mm(small_mirror, jnp.concatenate([term[1, j] for j in range(terms)], 1)).astype(bf16)
    for j in range(terms):
        term[1, j] = turned[:, j * cols : (j + 1) * cols]

    for copy in halo_copies:
        copy.wait()
    lane = lax.broadcasted_iota(jnp.int32, (2 * freq_count, cols), 1)
    keep_left = jnp.where((lane >= cols - radius) & (tile > 0), 1.0, 0.0)
    keep_right = jnp.where((lane < radius) & (tile < tiles - 1), 1.0, 0.0)
    around = jnp.concatenate([halo[0] * keep_left + halo[1] * keep_right, own_spec[...]], 1)
    t = mm3(split(around), (direct[0], direct[1]))
    a_re = t[:freq_count, :ring] + t[freq_count:, ring:]
    a_im = t[freq_count:, :ring] - t[:freq_count, ring:]
    products = []
    for k in range(kernels):
        g_re, g_im = gains[k, :, :ring], gains[k, :, ring:]
        products.append(jnp.concatenate([a_re * g_re - a_im * g_im, a_re * g_im + a_im * g_re], 1))
    loads[3].wait()
    band = mm3(split(jnp.concatenate(products, 0)), (back[0], back[1]))
    for k in range(kernels):
        high, low = split(band[k * freq_count : (k + 1) * freq_count])
        for part in range(2):
            at = (part * kernels + k) * cols
            source = slice(part * cols, (part + 1) * cols)
            stacked[:freq_count, at : at + cols] = high[:, source]
            stacked[freq_count : 2 * freq_count, at : at + cols] = high[:, source]
            stacked[2 * freq_count :, at : at + cols] = low[:, source]

    def image_copy(d):
        return pltpu.make_async_remote_copy(
            src_ref=own_image.at[after(d)], dst_ref=images.at[d], send_sem=image_send.at[d],
            recv_sem=image_recv.at[d], device_id=(tile, after(d)), device_id_type=MESH,
        )

    dose = 1.0 + 0.1 * level(node_index[1, node])
    side = kernels * cols
    cos_part[...] = mm(cos_in[...], stacked[...])
    sin_part[...] = mm(sin_in[...], stacked[...])

    def fields(row, count, k):
        p = cos_part[pl.ds(row, count), k * cols : (k + 1) * cols]
        t = cos_part[pl.ds(row, count), side + k * cols : side + (k + 1) * cols]
        r = sin_part[pl.ds(row, count), k * cols : (k + 1) * cols]
        q = sin_part[pl.ds(row, count), side + k * cols : side + (k + 1) * cols]
        return p - q, r + t, p + q, t - r

    piece = images.shape[3]
    parts = chunk // piece

    @pl.loop(0, nodes)
    def _(i):
        d = lax.rem(i + 1, nodes)
        mine = after(d)

        @pl.loop(0, parts)
        def _(part):
            at = pl.multiple_of(mine * chunk + part * piece, piece)
            first = jnp.zeros((piece, cols), f32)
            second = jnp.zeros((piece, cols), f32)
            for k in range(kernels):
                a, b, c, e = fields(at, piece, k)
                weight = kernel_weights[0, k]
                first = first + weight * (a * a + b * b)
                second = second + weight * (c * c + e * e)
            for h, intensity in ((0, first), (1, second)):
                value = jax.nn.sigmoid(resist_slope * (dose * intensity - resist_level))
                resist[h, pl.ds(at, piece), :] = value
                own_image[mine, part, h] = value.astype(bf16)

        @pl.when(d != 0)
        def _():
            image_copy(d).start()

    images[0] = own_image[node]

    sources = [before(d) for d in range(nodes)]
    bases = [basis_of(node_index, n) for n in sources]
    weights = [node_weights[n] for n in sources]
    scaled = [[weights[d] * b for b in bases[d]] for d in range(nodes)]
    for d in range(1, nodes):
        image_copy(d).wait()

    def push_copy(d, part):
        return pltpu.make_async_remote_copy(
            src_ref=push.at[d, part], dst_ref=pressure.at[d, part], send_sem=push_send.at[d, part],
            recv_sem=push_recv.at[d, part], device_id=(tile, before(d)), device_id_type=MESH,
        )

    @pl.loop(0, parts)
    def _(part):
        @pl.loop(0, 2)
        def _(h):
            seen = [images[d, part, h].astype(f32) for d in range(nodes)]
            sums = [None] * nodes
            for j in range(terms):
                coefficient = scaled[0][j] * seen[0]
                for d in range(1, nodes):
                    coefficient = coefficient + scaled[d][j] * seen[d]
                wanted = term[h, j, pl.ds(pl.multiple_of(part * piece, piece), piece), :]
                mixed = chaos_weights[j] * jnp.tanh(coefficient - wanted.astype(f32))
                for d in range(nodes):
                    one = scaled[d][j] * mixed
                    sums[d] = one if sums[d] is None else sums[d] + one
            for d in range(nodes):
                if d:
                    push[d, part, h] = sums[d]
                else:
                    pressure[0, part, h] = sums[d]

        for d in range(1, nodes):
            push_copy(d, part).start()

    @pl.loop(0, nodes)
    def _(d):
        @pl.loop(0, parts)
        def _(part):
            @pl.when(d != 0)
            def _():
                push_copy(d, part).wait()

            at = pl.multiple_of(after(d) * chunk + part * piece, piece)
            slopes = []
            for h in range(2):
                value = resist[h, pl.ds(at, piece), :]
                slopes.append(pressure[d, part, h] * value * (1.0 - value) * (resist_slope * dose))
            for k in range(kernels):
                a, b, c, e = fields(at, piece, k)
                a, b, c, e = a * slopes[0], b * slopes[0], c * slopes[1], e * slopes[1]
                for base, where, value in ((0, 0, a + c), (0, side, b + e), (half, 0, b - e), (half, side, c - a)):
                    high, low = split(value)
                    lanes = slice(where + k * cols, where + (k + 1) * cols)
                    dfield[0, pl.ds(base + at, piece), lanes] = high
                    dfield[1, pl.ds(base + at, piece), lanes] = low

    both = trans[...].reshape(2 * freq_count, 2 * half)
    t = mm(both, dfield[0])
    dband = t[:freq_count] + t[freq_count:] + mm(trans[0], dfield[1])
    pieces = []
    for k in range(kernels):
        one = jnp.concatenate([dband[:, k * cols : (k + 1) * cols], dband[:, side + k * cols : side + (k + 1) * cols]], 1)
        pieces.append(one * (2.0 * kernel_weights[0, k]))
    loads[4].wait()
    t = mm3(split(jnp.concatenate(pieces, 0)), (back_t[0], back_t[1]))
    z_re = jnp.zeros((freq_count, ring), f32)
    z_im = jnp.zeros((freq_count, ring), f32)
    for k in range(kernels):
        d_re = t[k * freq_count : (k + 1) * freq_count, :ring]
        d_im = t[k * freq_count : (k + 1) * freq_count, ring:]
        g_re, g_im = gains[k, :, :ring], gains[k, :, ring:]
        z_re = z_re + (g_re * d_re + g_im * d_im)
        z_im = z_im + (g_re * d_im - g_im * d_re)
    t = mm3(split(jnp.concatenate([z_re, z_im], 0)), (direct[0], direct[1]))
    dspec = jnp.concatenate(
        [t[:freq_count, :ring] - t[freq_count:, ring:], t[:freq_count, ring:] + t[freq_count:, :ring]], 0
    )
    for n in range(nodes):
        for block in range(2):
            dparts[n, block] = dspec[n * share : (n + 1) * share, block * cols : (block + 1) * cols]

    def z_copy(d):
        return pltpu.make_async_remote_copy(
            src_ref=dparts.at[after(d), 1], dst_ref=zin.at[d], send_sem=z_send.at[d],
            recv_sem=z_recv.at[d], device_id=(tile, after(d)), device_id_type=MESH,
        )

    def e_copy(d, side_id):
        to = right if side_id == 0 else left
        return pltpu.make_async_remote_copy(
            src_ref=dparts.at[after(d), 0], dst_ref=ein.at[side_id, d], send_sem=e_send.at[side_id, d],
            recv_sem=e_recv.at[side_id, d], device_id=(to, after(d)), device_id_type=MESH,
        )

    copies = []
    for d in range(nodes):
        copies += [e_copy(d, 0), e_copy(d, 1)]
        if d:
            copies.append(z_copy(d))
    for copy in copies:
        copy.start()
    for copy in copies:
        copy.wait()
    lane = lax.broadcasted_iota(jnp.int32, (share, cols), 1)
    keep_left = jnp.where((lane < radius) & (tile > 0), 1.0, 0.0)
    keep_right = jnp.where((lane >= cols - radius) & (tile < tiles - 1), 1.0, 0.0)
    value = dparts[node, 1]
    for d in range(nodes):
        if d:
            value = value + zin[d]
        value = value + ein[0, d] * keep_left + ein[1, d] * keep_right
    total[...] = value
    gathered[node] = value

    def g_copy(d):
        return pltpu.make_async_remote_copy(
            src_ref=total, dst_ref=gathered.at[node], send_sem=g_send.at[d],
            recv_sem=g_recv.at[d], device_id=(tile, after(d)), device_id_type=MESH,
        )

    for d in range(1, nodes):
        g_copy(d).start()
    for d in range(1, nodes):
        g_copy(d).wait()
    summed = jnp.concatenate([gathered[n] for n in range(nodes)], 0)
    out[...] = mm3((own_table[0], own_table[1]), split(summed))


def local(
    tiles, nodes,
    mask_field, kernel_taps, kernel_weights, node_weights, node_index, freq_index, chaos_weights, target,
):
    rows, cols = mask_field.shape
    _, kernels, _, freq_count, tap_count = kernel_taps.shape
    radius = (tap_count - 1) // 2
    half, chunk = rows // 2, rows // 2 // nodes
    terms = chaos_weights.shape[0]
    ring = 2 * cols
    share = 2 * freq_count // nodes
    piece = min(32, chunk)
    direct, back, back_t = column_tables(cols, radius, freq_count)
    vmem = pl.BlockSpec(memory_space=pltpu.VMEM)
    smem = pl.BlockSpec(memory_space=pltpu.SMEM)
    hbm = pl.BlockSpec(memory_space=pl.ANY)
    scratch = pltpu.VMEM
    dma = pltpu.SemaphoreType.DMA
    return pl.pallas_call(
        functools.partial(kernel, tiles, nodes, radius),
        out_shape=jax.ShapeDtypeStruct((rows // nodes, cols), f32),
        in_specs=[hbm, hbm, smem, smem, smem, smem, smem, hbm, hbm, hbm, hbm],
        out_specs=vmem,
        scratch_shapes=[
            scratch((rows, cols), f32),
            scratch((2 * kernels, freq_count, tap_count), f32),
            scratch(direct.shape, bf16),
            scratch(back.shape, bf16),
            scratch(back_t.shape, bf16),
            scratch((freq_count, 128), jnp.int32),
            scratch((8, 256), jnp.int32),
            scratch((half, 3 * freq_count), bf16),
            scratch((half, 3 * freq_count), bf16),
            scratch((2, freq_count, 2 * half), bf16),
            scratch((2, rows // nodes, 2 * freq_count), bf16),
            scratch((2 * kernels * freq_count, 128), f32),
            scratch((kernels, freq_count, 2 * ring), f32),
            scratch((2 * freq_count, cols), f32),
            scratch((2, 2 * freq_count, cols), f32),
            scratch((3 * freq_count, 2 * kernels * cols), bf16),
            scratch((half, 2 * kernels * cols), f32),
            scratch((half, 2 * kernels * cols), f32),
            scratch((2, half, cols), f32),
            scratch((nodes, chunk // piece, 2, piece, cols), bf16),
            scratch((nodes, chunk // piece, 2, piece, cols), bf16),
            scratch((2, terms, chunk, cols), bf16),
            scratch((nodes, chunk // piece, 2, piece, cols), f32),
            scratch((nodes, chunk // piece, 2, piece, cols), f32),
            scratch((2, 2 * half, 2 * kernels * cols), bf16),
            scratch((nodes, 2, share, cols), f32),
            scratch((nodes, share, cols), f32),
            scratch((2, nodes, share, cols), f32),
            scratch((share, cols), f32),
            scratch((nodes, share, cols), f32),
            dma((7,)), dma((2,)), dma((2,)),
            dma((nodes,)), dma((nodes,)), dma((nodes, chunk // piece)), dma((nodes, chunk // piece)),
            dma((nodes,)), dma((nodes,)), dma((2, nodes)), dma((2, nodes)),
            dma((nodes,)), dma((nodes,)),
        ],
        compiler_params=pltpu.CompilerParams(
            collective_id=0, has_side_effects=True, vmem_limit_bytes=63 * 1024 * 1024
        ),
        name="mask_gradient",
    )(
        mask_field, kernel_taps.reshape(2 * kernels, freq_count, tap_count), kernel_weights, node_weights,
        node_index.T, freq_index, chaos_weights, target, direct, back, back_t,
    )


def solution(mesh):
    placed = (
        P(None, "tile"),
        P("node", None, None, None, None),
        P("node", None),
        P(),
        P(),
        P(),
        P(),
        P(None, None, "tile"),
    )
    return jax.shard_map(
        functools.partial(local, mesh.shape["tile"], mesh.shape["node"]),
        mesh=mesh, in_specs=placed, out_specs=P("node", "tile"), check_vma=False,
    )
```

```python
import functools
import math

import jax
import jax.numpy as jnp
import ml_dtypes
import numpy as np
from jax import lax
from jax.experimental import pallas as pl
from jax.experimental.pallas import tpu as pltpu
from jax.sharding import PartitionSpec as P

LEVELS = 5
DEGREES = 5
MESH = pl.DeviceIdType.MESH
bf16 = jnp.bfloat16
f32 = jnp.float32
resist_slope = 4.0
resist_level = 0.6


def split(value):
    high = value.astype(bf16)
    return high, (value - high.astype(f32)).astype(bf16)


def mm(left, right):
    return jnp.dot(left, right, preferred_element_type=f32)


def mm3(left, right):
    count = left[0].shape[0]
    both = mm(jnp.concatenate(left, 0), right[0])
    return both[:count] + (mm(left[0], right[1]) + both[count:])


def half_turn_cosine(step, half):
    folded = jnp.abs((step & (2 * half - 1)) - half).astype(f32)
    t = folded * (2.0 / half) - 1.0
    s = t * t
    acc = jnp.full_like(t, 5.6921729e-8)
    for c in (-3.5988432e-6, 1.6044118e-4, -4.6817541e-3, 7.9692626e-2, -0.64596410, 1.57079633):
        acc = acc * s + c
    return acc * t


def encode(value):
    scaled = value * 2.0**20
    square = scaled * scaled
    fourth = square * square
    return jnp.where(value < 0.0, -fourth, fourth).astype(bf16)


def decode(code):
    code = code.astype(f32)
    size = jnp.sqrt(jnp.sqrt(jnp.abs(code))) * 2.0**-20
    return jnp.where(code < 0.0, -size, size)


def legendre(u):
    s = u * u
    return [None, u, 1.5 * s - 0.5, (2.5 * s - 1.5) * u, (4.375 * s - 3.75) * s + 0.375]


def level(index):
    return index.astype(f32) * (2.0 / (LEVELS - 1)) - 1.0


def basis_of(node_index, node):
    focus = legendre(level(node_index[0, node]))
    dose = legendre(level(node_index[1, node]))
    terms = []
    for degree in range(DEGREES):
        for p in range(degree, -1, -1):
            a, b = focus[p], dose[degree - p]
            terms.append(1.0 if a is None and b is None else b if a is None else a if b is None else a * b)
    return terms


def column_tables(cols, radius, freq_count):
    ring = 2 * cols
    w = np.arange(ring)
    angle = 2 * np.pi * ((w[:, None] * w[None, :]) % ring) / ring
    direct = np.concatenate([np.cos(angle), np.sin(angle)], 1)
    out = 2 * np.pi * ((w[:, None] * (np.arange(cols) + cols - radius)[None, :]) % ring) / ring
    c, s = np.cos(out), np.sin(out)
    back = np.concatenate([np.concatenate([c, s], 1), np.concatenate([-s, c], 1)], 0)
    back = back / (ring * math.sqrt(freq_count))
    pieces = []
    for table in (direct, back, back.T):
        high = table.astype(ml_dtypes.bfloat16)
        low = (table - high.astype(np.float64)).astype(ml_dtypes.bfloat16)
        pieces.append(np.stack([high, low]))
    return pieces


def kernel(
    tiles, nodes, radius,
    mask_hbm, taps_hbm, kernel_weights_hbm, node_weights_hbm, node_index_hbm, freq_hbm, chaos_weights_hbm, target,
    direct_hbm, back_hbm, back_t_hbm,
    out,
    kernel_weights, node_weights, node_index, freq, chaos_weights,
    mask, taps, direct, back, back_t,
    freq_rows, freq_lanes, cos_in, sin_in, trans, own_table, padded_taps, gains,
    own_spec, halo, stacked, cos_part, sin_part, resist, own_image, images, term,
    push, pressure, own_pressure, given, dfield, dparts, dedges, zin, ein, total, gathered,
    local_sem, halo_send, halo_recv, image_send, image_recv, push_send, push_recv,
    z_send, z_recv, e_send, e_recv, g_send, g_recv,
):
    tile, node = lax.axis_index("tile"), lax.axis_index("node")
    right, left = lax.rem(tile + 1, tiles), lax.rem(tile + tiles - 1, tiles)
    rows, cols = mask.shape
    half = rows // 2
    chunk = half // nodes
    freq_count = freq.shape[0]
    terms = chaos_weights.shape[0]
    kernels = taps.shape[0] // 2
    share = 2 * freq_count // nodes

    def after(d):
        return lax.rem(node + d, nodes)

    def before(d):
        return lax.rem(node + nodes - d, nodes)

    barrier = pltpu.get_barrier_semaphore()
    for d in range(1, nodes):
        pl.semaphore_signal(barrier, inc=1, device_id=(tile, after(d)), device_id_type=MESH)
    for d in range(nodes):
        pl.semaphore_signal(barrier, inc=1, device_id=(right, after(d)), device_id_type=MESH)
        pl.semaphore_signal(barrier, inc=1, device_id=(left, after(d)), device_id_type=MESH)

    loads = []
    for i, (source, held) in enumerate((
        (mask_hbm, mask), (direct_hbm, direct), (taps_hbm, taps), (back_hbm, back), (back_t_hbm, back_t),
        (kernel_weights_hbm, kernel_weights), (node_weights_hbm, node_weights),
        (node_index_hbm, node_index), (freq_hbm, freq), (chaos_weights_hbm, chaos_weights),
    )):
        loads.append(pltpu.make_async_copy(source, held, local_sem.at[i + 2]))
    for load in [loads[8]] + loads[:3] + loads[5:8] + loads[9:]:
        load.start()
    upper = pltpu.make_async_copy(
        target.at[:, pl.ds(pl.multiple_of(node * chunk, chunk), chunk), :], term.at[0], local_sem.at[0]
    )
    lower = pltpu.make_async_copy(
        target.at[:, pl.ds(pl.multiple_of(rows - (node + 1) * chunk, chunk), chunk), :],
        term.at[1], local_sem.at[1],
    )
    upper.start()
    lower.start()
    for load in loads[3:5]:
        load.start()

    loads[8].wait()
    row_id = lax.broadcasted_iota(jnp.int32, freq_rows.shape, 0)
    lane_id = lax.broadcasted_iota(jnp.int32, freq_lanes.shape, 1) % freq_count
    by_row = jnp.zeros(freq_rows.shape, jnp.int32)
    by_lane = jnp.zeros(freq_lanes.shape, jnp.int32)
    for i in range(freq_count):
        by_row = jnp.where(row_id == i, freq[i], by_row)
        by_lane = jnp.where(lane_id == i, freq[i], by_lane)
    freq_rows[...] = by_row
    freq_lanes[...] = by_lane

    place = lax.broadcasted_iota(jnp.int32, (freq_count, half), 1)
    step = freq_rows[:, :1] * (2 * place + 1)
    c_high, c_low = split(half_turn_cosine(step, rows))
    s_high, s_low = split(half_turn_cosine(step - half, rows))
    trans[0, :, :half] = c_high
    trans[1, :, :half] = c_low
    trans[0, :, half:] = s_high
    trans[1, :, half:] = s_low

    ri = lax.broadcasted_iota(jnp.int32, (half, half), 0)
    ci = lax.broadcasted_iota(jnp.int32, (half, half), 1)
    mirror = jnp.where(ri + ci == half - 1, 1.0, 0.0).astype(bf16)
    loads[0].wait()
    m_high, m_low = split(mask[half:, :])
    mirrored = mm(mirror, m_high) + mm(mirror, m_low)
    top = mask[:half, :]
    norm = 1.0 / math.sqrt(rows)
    own_spec[:freq_count, :] = mm3((c_high, c_low), split(top + mirrored)) * norm
    own_spec[freq_count:, :] = mm3((s_high, s_low), split(top - mirrored)) * -norm

    pl.semaphore_wait(barrier, 3 * nodes - 1)
    halo_copies = []
    for side, to in ((0, right), (1, left)):
        halo_copies.append(pltpu.make_async_remote_copy(
            src_ref=own_spec, dst_ref=halo.at[side], send_sem=halo_send.at[side],
            recv_sem=halo_recv.at[side], device_id=(to, node), device_id_type=MESH,
        ))
        halo_copies[-1].start()

    wide = 3 * freq_count
    place = lax.broadcasted_iota(jnp.int32, (half, wide), 0)
    lane = lax.broadcasted_iota(jnp.int32, (half, wide), 1)
    middle = (lane >= freq_count) & (lane < 2 * freq_count)
    step = freq_lanes[:1, :wide] * (2 * place + 1)
    for table, value in ((cos_in, half_turn_cosine(step, rows)), (sin_in, half_turn_cosine(step - half, rows))):
        rounded = value.astype(bf16).astype(f32)
        table[...] = jnp.where(middle, value - rounded, rounded).astype(bf16)

    own_rows = rows // nodes
    place = lax.broadcasted_iota(jnp.int32, (own_rows, 2 * freq_count), 0) + node * own_rows
    lane = lax.broadcasted_iota(jnp.int32, (own_rows, 2 * freq_count), 1)
    step = freq_lanes[:1, : 2 * freq_count] * (2 * place + 1)
    step = jnp.where(lane < freq_count, step, step + half)
    own_table[0], own_table[1] = split(half_turn_cosine(step, rows) * norm)

    padded_taps[...] = jnp.zeros(padded_taps.shape, f32)
    loads[1].wait()
    loads[2].wait()
    for i in range(2 * kernels):
        padded_taps[i * freq_count : (i + 1) * freq_count, : 2 * radius + 1] = taps[i]
    near = padded_taps.shape[1]
    t = mm3(split(padded_taps[...]), (direct[0, :near, :], direct[1, :near, :]))
    ring = 2 * cols
    for k in range(kernels):
        re = t[2 * k * freq_count : (2 * k + 1) * freq_count]
        im = t[(2 * k + 1) * freq_count : (2 * k + 2) * freq_count]
        gains[k, :, :ring] = re[:, :ring] - im[:, ring:]
        gains[k, :, ring:] = re[:, ring:] + im[:, :ring]

    ri = lax.broadcasted_iota(jnp.int32, (chunk, chunk), 0)
    ci = lax.broadcasted_iota(jnp.int32, (chunk, chunk), 1)
    small_mirror = jnp.where(ri + ci == chunk - 1, 1.0, 0.0).astype(bf16)
    upper.wait()
    lower.wait()
    turned = mm(small_mirror, jnp.concatenate([term[1, j] for j in range(terms)], 1)).astype(bf16)
    for j in range(terms):
        term[1, j] = turned[:, j * cols : (j + 1) * cols]

    for copy in halo_copies:
        copy.wait()
    lane = lax.broadcasted_iota(jnp.int32, (2 * freq_count, cols), 1)
    keep_left = jnp.where((lane >= cols - radius) & (tile > 0), 1.0, 0.0)
    keep_right = jnp.where((lane < radius) & (tile < tiles - 1), 1.0, 0.0)
    around = jnp.concatenate([halo[0] * keep_left + halo[1] * keep_right, own_spec[...]], 1)
    t = mm3(split(around), (direct[0], direct[1]))
    a_re = t[:freq_count, :ring] + t[freq_count:, ring:]
    a_im = t[freq_count:, :ring] - t[:freq_count, ring:]
    products = []
    for k in range(kernels):
        g_re, g_im = gains[k, :, :ring], gains[k, :, ring:]
        products.append(jnp.concatenate([a_re * g_re - a_im * g_im, a_re * g_im + a_im * g_re], 1))
    loads[3].wait()
    band = mm3(split(jnp.concatenate(products, 0)), (back[0], back[1]))
    for k in range(kernels):
        high, low = split(band[k * freq_count : (k + 1) * freq_count])
        for part in range(2):
            at = (part * kernels + k) * cols
            source = slice(part * cols, (part + 1) * cols)
            stacked[:freq_count, at : at + cols] = high[:, source]
            stacked[freq_count : 2 * freq_count, at : at + cols] = high[:, source]
            stacked[2 * freq_count :, at : at + cols] = low[:, source]

    def image_copy(d, part):
        return pltpu.make_async_remote_copy(
            src_ref=own_image.at[after(d), part], dst_ref=images.at[d, part], send_sem=image_send.at[d, part],
            recv_sem=image_recv.at[d, part], device_id=(tile, after(d)), device_id_type=MESH,
        )

    for load in loads[5:8] + loads[9:]:
        load.wait()
    dose = 1.0 + 0.1 * level(node_index[1, node])
    side = kernels * cols
    cos_part[...] = mm(cos_in[...], stacked[...])
    sin_part[...] = mm(sin_in[...], stacked[...])

    def fields(row, count, k):
        p = cos_part[pl.ds(row, count), k * cols : (k + 1) * cols]
        t = cos_part[pl.ds(row, count), side + k * cols : side + (k + 1) * cols]
        r = sin_part[pl.ds(row, count), k * cols : (k + 1) * cols]
        q = sin_part[pl.ds(row, count), side + k * cols : side + (k + 1) * cols]
        return p - q, r + t, p + q, t - r

    piece = images.shape[3]
    parts = chunk // piece

    @pl.loop(0, parts)
    def _(part):
        @pl.loop(0, nodes)
        def _(i):
            d = lax.rem(i + 1, nodes)
            mine = after(d)
            at = pl.multiple_of(mine * chunk + part * piece, piece)
            first = jnp.zeros((piece, cols), f32)
            second = jnp.zeros((piece, cols), f32)
            for k in range(kernels):
                a, b, c, e = fields(at, piece, k)
                weight = kernel_weights[0, k]
                first = first + weight * (a * a + b * b)
                second = second + weight * (c * c + e * e)
            for h, intensity in ((0, first), (1, second)):
                value = jax.nn.sigmoid(resist_slope * (dose * intensity - resist_level))
                resist[h, pl.ds(at, piece), :] = value
                own_image[mine, part, h] = value.astype(bf16)

            @pl.when(d != 0)
            def _():
                image_copy(d, part).start()

    images[0] = own_image[node]

    sources = [before(d) for d in range(nodes)]
    bases = [basis_of(node_index, n) for n in sources]
    weights = [node_weights[n] for n in sources]
    scaled = [[weights[d] * b for b in bases[d]] for d in range(nodes)]

    def push_copy(d, part):
        return pltpu.make_async_remote_copy(
            src_ref=push.at[d, part], dst_ref=pressure.at[d, part], send_sem=push_send.at[d, part],
            recv_sem=push_recv.at[d, part], device_id=(tile, before(d)), device_id_type=MESH,
        )

    @pl.loop(0, parts)
    def _(part):
        for d in range(1, nodes):
            image_copy(d, part).wait()

        @pl.loop(0, 2)
        def _(h):
            seen = [images[d, part, h].astype(f32) for d in range(nodes)]
            sums = [None] * nodes
            for j in range(terms):
                coefficient = scaled[0][j] * seen[0]
                for d in range(1, nodes):
                    coefficient = coefficient + scaled[d][j] * seen[d]
                wanted = term[h, j, pl.ds(pl.multiple_of(part * piece, piece), piece), :]
                mixed = chaos_weights[j] * jnp.tanh(coefficient - wanted.astype(f32))
                for d in range(nodes):
                    one = scaled[d][j] * mixed
                    sums[d] = one if sums[d] is None else sums[d] + one
            for d in range(nodes):
                if d:
                    push[d, part, h] = encode(sums[d])
                else:
                    own_pressure[part, h] = sums[d]

        for d in range(1, nodes):
            push_copy(d, part).start()

    @pl.loop(0, parts)
    def _(part):
        @pl.loop(0, nodes)
        def _(d):
            @pl.when(d == 0)
            def _():
                given[...] = own_pressure[part]

            @pl.when(d != 0)
            def _():
                push_copy(d, part).wait()
                given[...] = decode(pressure[d, part])

            at = pl.multiple_of(after(d) * chunk + part * piece, piece)
            slopes = []
            for h in range(2):
                value = resist[h, pl.ds(at, piece), :]
                slopes.append(given[h] * value * (1.0 - value) * (resist_slope * dose))
            for k in range(kernels):
                a, b, c, e = fields(at, piece, k)
                a, b, c, e = a * slopes[0], b * slopes[0], c * slopes[1], e * slopes[1]
                for base, where, value in ((0, 0, a + c), (0, side, b + e), (half, 0, b - e), (half, side, c - a)):
                    high, low = split(value)
                    lanes = slice(where + k * cols, where + (k + 1) * cols)
                    dfield[0, pl.ds(base + at, piece), lanes] = high
                    dfield[1, pl.ds(base + at, piece), lanes] = low

    both = trans[...].reshape(2 * freq_count, 2 * half)
    t = mm(both, dfield[0])
    dband = t[:freq_count] + t[freq_count:] + mm(trans[0], dfield[1])
    pieces = []
    for k in range(kernels):
        one = jnp.concatenate([dband[:, k * cols : (k + 1) * cols], dband[:, side + k * cols : side + (k + 1) * cols]], 1)
        pieces.append(one * (2.0 * kernel_weights[0, k]))
    loads[4].wait()
    t = mm3(split(jnp.concatenate(pieces, 0)), (back_t[0], back_t[1]))
    z_re = jnp.zeros((freq_count, ring), f32)
    z_im = jnp.zeros((freq_count, ring), f32)
    for k in range(kernels):
        d_re = t[k * freq_count : (k + 1) * freq_count, :ring]
        d_im = t[k * freq_count : (k + 1) * freq_count, ring:]
        g_re, g_im = gains[k, :, :ring], gains[k, :, ring:]
        z_re = z_re + (g_re * d_re + g_im * d_im)
        z_im = z_im + (g_re * d_im - g_im * d_re)
    t = mm3(split(jnp.concatenate([z_re, z_im], 0)), (direct[0], direct[1]))
    dspec = jnp.concatenate(
        [t[:freq_count, :ring] - t[freq_count:, ring:], t[:freq_count, ring:] + t[freq_count:, :ring]], 0
    )
    fold = ein.shape[2]
    groups = share // fold
    lane = lax.broadcasted_iota(jnp.int32, (fold, cols), 1)
    for n in range(nodes):
        dparts[n] = dspec[n * share : (n + 1) * share, cols:]
        for side_id in range(2):
            packed = None
            for g in range(groups):
                block = dspec[n * share + g * fold : n * share + (g + 1) * fold, :cols]
                if g == 0:
                    packed = block
                    continue
                moved = pltpu.roll(block, g * radius if side_id == 0 else cols - g * radius, 1)
                there = lane >= g * radius if side_id == 0 else lane < cols - g * radius
                packed = jnp.where(there, moved, packed)
            dedges[side_id, n] = packed

    def z_copy(d):
        return pltpu.make_async_remote_copy(
            src_ref=dparts.at[after(d)], dst_ref=zin.at[d], send_sem=z_send.at[d],
            recv_sem=z_recv.at[d], device_id=(tile, after(d)), device_id_type=MESH,
        )

    def e_copy(d, side_id):
        to = right if side_id == 0 else left
        return pltpu.make_async_remote_copy(
            src_ref=dedges.at[side_id, after(d)], dst_ref=ein.at[side_id, d], send_sem=e_send.at[side_id, d],
            recv_sem=e_recv.at[side_id, d], device_id=(to, after(d)), device_id_type=MESH,
        )

    copies = []
    for d in range(nodes):
        copies += [e_copy(d, 0), e_copy(d, 1)]
        if d:
            copies.append(z_copy(d))
    for copy in copies:
        copy.start()
    for copy in copies:
        copy.wait()
    value = dparts[node]
    from_left, from_right = ein[0, 0], ein[1, 0]
    for d in range(1, nodes):
        value = value + zin[d]
        from_left, from_right = from_left + ein[0, d], from_right + ein[1, d]
    keep_left = jnp.where((lane < radius) & (tile > 0), 1.0, 0.0)
    keep_right = jnp.where((lane >= cols - radius) & (tile < tiles - 1), 1.0, 0.0)
    edges = []
    for g in range(groups):
        a, b = from_left, from_right
        if g:
            a, b = pltpu.roll(a, cols - g * radius, 1), pltpu.roll(b, g * radius, 1)
        edges.append(a * keep_left + b * keep_right)
    value = value + jnp.concatenate(edges, 0)
    total[...] = value
    gathered[node] = value

    def g_copy(d):
        return pltpu.make_async_remote_copy(
            src_ref=total, dst_ref=gathered.at[node], send_sem=g_send.at[d],
            recv_sem=g_recv.at[d], device_id=(tile, after(d)), device_id_type=MESH,
        )

    for d in range(1, nodes):
        g_copy(d).start()
    for d in range(1, nodes):
        g_copy(d).wait()
    summed = jnp.concatenate([gathered[n] for n in range(nodes)], 0)
    out[...] = mm3((own_table[0], own_table[1]), split(summed))


def local(
    tiles, nodes,
    mask_field, kernel_taps, kernel_weights, node_weights, node_index, freq_index, chaos_weights, target,
):
    rows, cols = mask_field.shape
    _, kernels, _, freq_count, tap_count = kernel_taps.shape
    radius = (tap_count - 1) // 2
    half, chunk = rows // 2, rows // 2 // nodes
    terms = chaos_weights.shape[0]
    ring = 2 * cols
    share = 2 * freq_count // nodes
    piece = min(32, chunk)
    fold = 8 if share % 8 == 0 and share // 8 * radius <= cols else share
    direct, back, back_t = column_tables(cols, radius, freq_count)
    vmem = pl.BlockSpec(memory_space=pltpu.VMEM)
    hbm = pl.BlockSpec(memory_space=pl.ANY)
    smem = pltpu.SMEM
    scratch = pltpu.VMEM
    dma = pltpu.SemaphoreType.DMA
    return pl.pallas_call(
        functools.partial(kernel, tiles, nodes, radius),
        out_shape=jax.ShapeDtypeStruct((rows // nodes, cols), f32),
        in_specs=[hbm] * 11,
        out_specs=vmem,
        scratch_shapes=[
            smem(kernel_weights.shape, f32),
            smem(node_weights.shape, f32),
            smem(node_index.shape[::-1], jnp.int32),
            smem(freq_index.shape, jnp.int32),
            smem(chaos_weights.shape, f32),
            scratch((rows, cols), f32),
            scratch((2 * kernels, freq_count, tap_count), f32),
            scratch(direct.shape, bf16),
            scratch(back.shape, bf16),
            scratch(back_t.shape, bf16),
            scratch((freq_count, 128), jnp.int32),
            scratch((8, 256), jnp.int32),
            scratch((half, 3 * freq_count), bf16),
            scratch((half, 3 * freq_count), bf16),
            scratch((2, freq_count, 2 * half), bf16),
            scratch((2, rows // nodes, 2 * freq_count), bf16),
            scratch((2 * kernels * freq_count, 128), f32),
            scratch((kernels, freq_count, 2 * ring), f32),
            scratch((2 * freq_count, cols), f32),
            scratch((2, 2 * freq_count, cols), f32),
            scratch((3 * freq_count, 2 * kernels * cols), bf16),
            scratch((half, 2 * kernels * cols), f32),
            scratch((half, 2 * kernels * cols), f32),
            scratch((2, half, cols), f32),
            scratch((nodes, chunk // piece, 2, piece, cols), bf16),
            scratch((nodes, chunk // piece, 2, piece, cols), bf16),
            scratch((2, terms, chunk, cols), bf16),
            scratch((nodes, chunk // piece, 2, piece, cols), bf16),
            scratch((nodes, chunk // piece, 2, piece, cols), bf16),
            scratch((chunk // piece, 2, piece, cols), f32),
            scratch((2, piece, cols), f32),
            scratch((2, 2 * half, 2 * kernels * cols), bf16),
            scratch((nodes, share, cols), f32),
            scratch((2, nodes, fold, cols), f32),
            scratch((nodes, share, cols), f32),
            scratch((2, nodes, fold, cols), f32),
            scratch((share, cols), f32),
            scratch((nodes, share, cols), f32),
            dma((12,)), dma((2,)), dma((2,)),
            dma((nodes, chunk // piece)), dma((nodes, chunk // piece)), dma((nodes, chunk // piece)), dma((nodes, chunk // piece)),
            dma((nodes,)), dma((nodes,)), dma((2, nodes)), dma((2, nodes)),
            dma((nodes,)), dma((nodes,)),
        ],
        compiler_params=pltpu.CompilerParams(
            collective_id=0, has_side_effects=True, vmem_limit_bytes=63 * 1024 * 1024
        ),
        name="mask_gradient",
    )(
        mask_field, kernel_taps.reshape(2 * kernels, freq_count, tap_count), kernel_weights, node_weights,
        node_index.T, freq_index, chaos_weights, target, direct, back, back_t,
    )


def solution(mesh):
    placed = (
        P(None, "tile"),
        P("node", None, None, None, None),
        P("node", None),
        P(),
        P(),
        P(),
        P(),
        P(None, None, "tile"),
    )
    return jax.shard_map(
        functools.partial(local, mesh.shape["tile"], mesh.shape["node"]),
        mesh=mesh, in_specs=placed, out_specs=P("node", "tile"), check_vma=False,
    )
```

```python
import functools
import math

import jax
import jax.numpy as jnp
import ml_dtypes
import numpy as np
from jax import lax
from jax.experimental import pallas as pl
from jax.experimental.pallas import tpu as pltpu
from jax.sharding import PartitionSpec as P

LEVELS = 5
DEGREES = 5
MESH = pl.DeviceIdType.MESH
bf16 = jnp.bfloat16
f32 = jnp.float32
resist_slope = 4.0
resist_level = 0.6


def split(value):
    high = value.astype(bf16)
    return high, (value - high.astype(f32)).astype(bf16)


def mm(left, right):
    return jnp.dot(left, right, preferred_element_type=f32)


def mm3(left, right):
    count = left[0].shape[0]
    both = mm(jnp.concatenate(left, 0), right[0])
    return both[:count] + (mm(left[0], right[1]) + both[count:])


def half_turn_cosine(step, half):
    folded = jnp.abs((step & (2 * half - 1)) - half).astype(f32)
    t = folded * (2.0 / half) - 1.0
    s = t * t
    acc = jnp.full_like(t, 5.6921729e-8)
    for c in (-3.5988432e-6, 1.6044118e-4, -4.6817541e-3, 7.9692626e-2, -0.64596410, 1.57079633):
        acc = acc * s + c
    return acc * t


def encode(value):
    scaled = value * 2.0**20
    square = scaled * scaled
    fourth = square * square
    return jnp.where(value < 0.0, -fourth, fourth).astype(bf16)


def decode(code):
    code = code.astype(f32)
    size = jnp.sqrt(jnp.sqrt(jnp.abs(code))) * 2.0**-20
    return jnp.where(code < 0.0, -size, size)


def legendre(u):
    s = u * u
    return [None, u, 1.5 * s - 0.5, (2.5 * s - 1.5) * u, (4.375 * s - 3.75) * s + 0.375]


def level(index):
    return index.astype(f32) * (2.0 / (LEVELS - 1)) - 1.0


def basis_of(node_index, node):
    focus = legendre(level(node_index[0, node]))
    dose = legendre(level(node_index[1, node]))
    terms = []
    for degree in range(DEGREES):
        for p in range(degree, -1, -1):
            a, b = focus[p], dose[degree - p]
            terms.append(1.0 if a is None and b is None else b if a is None else a if b is None else a * b)
    return terms


def column_tables(cols, radius, freq_count):
    ring = 2 * cols
    w = np.arange(ring)
    angle = 2 * np.pi * ((w[:, None] * w[None, :]) % ring) / ring
    direct = np.concatenate([np.cos(angle), np.sin(angle)], 1)
    out = 2 * np.pi * ((w[:, None] * (np.arange(cols) + cols - radius)[None, :]) % ring) / ring
    c, s = np.cos(out), np.sin(out)
    back = np.concatenate([np.concatenate([c, s], 1), np.concatenate([-s, c], 1)], 0)
    back = back / (ring * math.sqrt(freq_count))
    pieces = []
    for table in (direct, back, back.T):
        high = table.astype(ml_dtypes.bfloat16)
        low = (table - high.astype(np.float64)).astype(ml_dtypes.bfloat16)
        pieces.append(np.stack([high, low]))
    return pieces


def kernel(
    tiles, nodes, radius,
    mask_hbm, taps_hbm, kernel_weights_hbm, node_weights_hbm, node_index_hbm, freq_hbm, chaos_weights_hbm, target,
    direct_hbm, back_hbm, back_t_hbm,
    out,
    kernel_weights, node_weights, node_index, freq, chaos_weights,
    mask, taps, direct, back, back_t,
    freq_rows, freq_lanes, row_table, scaled, trans, own_table, padded_taps, gains,
    own_spec, halo, stacked, parts_of, resist, own_image, images, term,
    push, pressure, own_pressure, given, dfield, dband, dparts, dedges, zin, ein, total, gathered,
    local_sem, halo_send, halo_recv, image_send, image_recv, push_send, push_recv,
    z_send, z_recv, e_send, e_recv, g_send, g_recv,
):
    tile, node = lax.axis_index("tile"), lax.axis_index("node")
    right, left = lax.rem(tile + 1, tiles), lax.rem(tile + tiles - 1, tiles)
    rows, cols = mask.shape
    half = rows // 2
    chunk = half // nodes
    freq_count = freq.shape[0]
    terms = chaos_weights.shape[0]
    kernels = taps.shape[0] // 2
    share = 2 * freq_count // nodes

    def after(d):
        return lax.rem(node + d, nodes)

    def before(d):
        return lax.rem(node + nodes - d, nodes)

    barrier = pltpu.get_barrier_semaphore()
    for d in range(1, nodes):
        pl.semaphore_signal(barrier, inc=1, device_id=(tile, after(d)), device_id_type=MESH)
    for d in range(nodes):
        pl.semaphore_signal(barrier, inc=1, device_id=(right, after(d)), device_id_type=MESH)
        pl.semaphore_signal(barrier, inc=1, device_id=(left, after(d)), device_id_type=MESH)

    loads = []
    for i, (source, held) in enumerate((
        (mask_hbm, mask), (direct_hbm, direct), (taps_hbm, taps), (back_hbm, back), (back_t_hbm, back_t),
        (kernel_weights_hbm, kernel_weights), (node_weights_hbm, node_weights),
        (node_index_hbm, node_index), (freq_hbm, freq), (chaos_weights_hbm, chaos_weights),
    )):
        loads.append(pltpu.make_async_copy(source, held, local_sem.at[i + 2]))
    for load in [loads[8]] + loads[:3] + loads[5:8] + loads[9:]:
        load.start()
    upper = pltpu.make_async_copy(
        target.at[:, pl.ds(pl.multiple_of(node * chunk, chunk), chunk), :], term.at[0], local_sem.at[0]
    )
    lower = pltpu.make_async_copy(
        target.at[:, pl.ds(pl.multiple_of(rows - (node + 1) * chunk, chunk), chunk), :],
        term.at[1], local_sem.at[1],
    )
    upper.start()
    lower.start()
    for load in loads[3:5]:
        load.start()

    loads[8].wait()
    row_id = lax.broadcasted_iota(jnp.int32, freq_rows.shape, 0)
    lane_id = lax.broadcasted_iota(jnp.int32, freq_lanes.shape, 1) % freq_count
    by_row = jnp.zeros(freq_rows.shape, jnp.int32)
    by_lane = jnp.zeros(freq_lanes.shape, jnp.int32)
    for i in range(freq_count):
        by_row = jnp.where(row_id == i, freq[i], by_row)
        by_lane = jnp.where(lane_id == i, freq[i], by_lane)
    freq_rows[...] = by_row
    freq_lanes[...] = by_lane

    place = lax.broadcasted_iota(jnp.int32, (freq_count, half), 1)
    step = freq_rows[:, :1] * (2 * place + 1)
    c_high, c_low = split(half_turn_cosine(step, rows))
    s_high, s_low = split(half_turn_cosine(step - half, rows))
    trans[0, :, :half] = c_high
    trans[1, :, :half] = c_low
    trans[0, :, half:] = s_high
    trans[1, :, half:] = s_low

    ri = lax.broadcasted_iota(jnp.int32, (half, half), 0)
    ci = lax.broadcasted_iota(jnp.int32, (half, half), 1)
    mirror = jnp.where(ri + ci == half - 1, 1.0, 0.0).astype(bf16)
    loads[0].wait()
    m_high, m_low = split(mask[half:, :])
    mirrored = mm(mirror, m_high) + mm(mirror, m_low)
    top = mask[:half, :]
    norm = 1.0 / math.sqrt(rows)
    own_spec[:freq_count, :] = mm3((c_high, c_low), split(top + mirrored)) * norm
    own_spec[freq_count:, :] = mm3((s_high, s_low), split(top - mirrored)) * -norm

    pl.semaphore_wait(barrier, 3 * nodes - 1)
    halo_copies = []
    for side, to in ((0, right), (1, left)):
        halo_copies.append(pltpu.make_async_remote_copy(
            src_ref=own_spec, dst_ref=halo.at[side], send_sem=halo_send.at[side],
            recv_sem=halo_recv.at[side], device_id=(to, node), device_id_type=MESH,
        ))
        halo_copies[-1].start()

    wide = 3 * freq_count
    strip = rows // 8
    lane = lax.broadcasted_iota(jnp.int32, (strip, wide), 1)
    middle = (lane >= freq_count) & (lane < 2 * freq_count)
    strip_row = lax.broadcasted_iota(jnp.int32, (strip, wide), 0)

    @pl.loop(0, 8)
    def _(i):
        sine = (i >= 4).astype(jnp.int32)
        place = strip_row + (i * strip - sine * half)
        value = half_turn_cosine(freq_lanes[:1, :wide] * (2 * place + 1) - sine * half, rows)
        rounded = value.astype(bf16).astype(f32)
        row_table[pl.ds(pl.multiple_of(i * strip, strip), strip), :] = jnp.where(
            middle, value - rounded, rounded
        ).astype(bf16)

    for load in loads[5:8] + loads[9:]:
        load.wait()
    for d in range(nodes):
        n = before(d)
        for j, b in enumerate(basis_of(node_index, n)):
            scaled[d, j] = node_weights[n] * b

    own_rows = rows // nodes
    place = lax.broadcasted_iota(jnp.int32, (own_rows, 2 * freq_count), 0) + node * own_rows
    lane = lax.broadcasted_iota(jnp.int32, (own_rows, 2 * freq_count), 1)
    step = freq_lanes[:1, : 2 * freq_count] * (2 * place + 1)
    step = jnp.where(lane < freq_count, step, step + half)
    own_table[0], own_table[1] = split(half_turn_cosine(step, rows) * norm)

    padded_taps[...] = jnp.zeros(padded_taps.shape, f32)
    loads[1].wait()
    loads[2].wait()
    for i in range(2 * kernels):
        padded_taps[i * freq_count : (i + 1) * freq_count, : 2 * radius + 1] = taps[i]
    near = padded_taps.shape[1]
    ring = 2 * cols
    run = 2 if kernels % 2 == 0 else 1

    @pl.loop(0, kernels // run)
    def _(i):
        height = 2 * run * freq_count
        rows_now = padded_taps[pl.ds(pl.multiple_of(i * height, height), height), :]
        t = mm3(split(rows_now), (direct[0, :near, :], direct[1, :near, :]))
        for k in range(run):
            re = t[2 * k * freq_count : (2 * k + 1) * freq_count]
            im = t[(2 * k + 1) * freq_count : (2 * k + 2) * freq_count]
            gains[i * run + k, :, :ring] = re[:, :ring] - im[:, ring:]
            gains[i * run + k, :, ring:] = re[:, ring:] + im[:, :ring]

    ri = lax.broadcasted_iota(jnp.int32, (chunk, chunk), 0)
    ci = lax.broadcasted_iota(jnp.int32, (chunk, chunk), 1)
    small_mirror = jnp.where(ri + ci == chunk - 1, 1.0, 0.0).astype(bf16)
    upper.wait()
    lower.wait()
    turned = mm(small_mirror, jnp.concatenate([term[1, j] for j in range(terms)], 1)).astype(bf16)
    for j in range(terms):
        term[1, j] = turned[:, j * cols : (j + 1) * cols]

    for copy in halo_copies:
        copy.wait()
    lane = lax.broadcasted_iota(jnp.int32, (2 * freq_count, cols), 1)
    keep_left = jnp.where((lane >= cols - radius) & (tile > 0), 1.0, 0.0)
    keep_right = jnp.where((lane < radius) & (tile < tiles - 1), 1.0, 0.0)
    around = jnp.concatenate([halo[0] * keep_left + halo[1] * keep_right, own_spec[...]], 1)
    t = mm3(split(around), (direct[0], direct[1]))
    a_re = t[:freq_count, :ring] + t[freq_count:, ring:]
    a_im = t[freq_count:, :ring] - t[:freq_count, ring:]
    products = []
    for k in range(kernels):
        g_re, g_im = gains[k, :, :ring], gains[k, :, ring:]
        products.append(jnp.concatenate([a_re * g_re - a_im * g_im, a_re * g_im + a_im * g_re], 1))
    loads[3].wait()
    band = mm3(split(jnp.concatenate(products, 0)), (back[0], back[1]))
    for k in range(kernels):
        high, low = split(band[k * freq_count : (k + 1) * freq_count])
        for part in range(2):
            at = (part * kernels + k) * cols
            source = slice(part * cols, (part + 1) * cols)
            stacked[:freq_count, at : at + cols] = high[:, source]
            stacked[freq_count : 2 * freq_count, at : at + cols] = high[:, source]
            stacked[2 * freq_count :, at : at + cols] = low[:, source]

    def image_copy(d, part):
        return pltpu.make_async_remote_copy(
            src_ref=own_image.at[after(d), part], dst_ref=images.at[d, part], send_sem=image_send.at[d, part],
            recv_sem=image_recv.at[d, part], device_id=(tile, after(d)), device_id_type=MESH,
        )

    dose = 1.0 + 0.1 * level(node_index[1, node])
    side = kernels * cols
    width = 4 * cols if 2 * kernels % 4 == 0 else side

    @pl.loop(0, 2 * side // width)
    def _(i):
        lanes = pl.ds(pl.multiple_of(i * width, width), width)
        parts_of[:, lanes] = mm(row_table[...], stacked[:, lanes])

    def fields(row, count, k):
        p = parts_of[pl.ds(row, count), k * cols : (k + 1) * cols]
        t = parts_of[pl.ds(row, count), side + k * cols : side + (k + 1) * cols]
        r = parts_of[pl.ds(half + row, count), k * cols : (k + 1) * cols]
        q = parts_of[pl.ds(half + row, count), side + k * cols : side + (k + 1) * cols]
        return p - q, r + t, p + q, t - r

    piece = images.shape[3]
    parts = chunk // piece

    @pl.loop(0, parts)
    def _(part):
        @pl.loop(0, nodes)
        def _(i):
            d = lax.rem(i + 1, nodes)
            mine = after(d)
            at = pl.multiple_of(mine * chunk + part * piece, piece)
            first = jnp.zeros((piece, cols), f32)
            second = jnp.zeros((piece, cols), f32)
            for k in range(kernels):
                a, b, c, e = fields(at, piece, k)
                weight = kernel_weights[0, k]
                first = first + weight * (a * a + b * b)
                second = second + weight * (c * c + e * e)
            for h, intensity in ((0, first), (1, second)):
                value = jax.nn.sigmoid(resist_slope * (dose * intensity - resist_level))
                resist[h, pl.ds(at, piece), :] = value
                own_image[mine, part, h] = value.astype(bf16)

            @pl.when(d != 0)
            def _():
                image_copy(d, part).start()

    images[0] = own_image[node]

    def push_copy(d, part):
        return pltpu.make_async_remote_copy(
            src_ref=push.at[d, part], dst_ref=pressure.at[d, part], send_sem=push_send.at[d, part],
            recv_sem=push_recv.at[d, part], device_id=(tile, before(d)), device_id_type=MESH,
        )

    @pl.loop(0, parts)
    def _(part):
        for d in range(1, nodes):
            image_copy(d, part).wait()

        @pl.loop(0, 2)
        def _(h):
            seen = [images[d, part, h].astype(f32) for d in range(nodes)]
            sums = [None] * nodes
            for j in range(terms):
                coefficient = scaled[0, j] * seen[0]
                for d in range(1, nodes):
                    coefficient = coefficient + scaled[d, j] * seen[d]
                wanted = term[h, j, pl.ds(pl.multiple_of(part * piece, piece), piece), :]
                mixed = chaos_weights[j] * jnp.tanh(coefficient - wanted.astype(f32))
                for d in range(nodes):
                    one = scaled[d, j] * mixed
                    sums[d] = one if sums[d] is None else sums[d] + one
            for d in range(nodes):
                if d:
                    push[d, part, h] = encode(sums[d])
                else:
                    own_pressure[part, h] = sums[d]

        for d in range(1, nodes):
            push_copy(d, part).start()

    @pl.loop(0, parts)
    def _(part):
        @pl.loop(0, nodes)
        def _(d):
            @pl.when(d == 0)
            def _():
                given[...] = own_pressure[part]

            @pl.when(d != 0)
            def _():
                push_copy(d, part).wait()
                given[...] = decode(pressure[d, part])

            at = pl.multiple_of(after(d) * chunk + part * piece, piece)
            slopes = []
            for h in range(2):
                value = resist[h, pl.ds(at, piece), :]
                slopes.append(given[h] * value * (1.0 - value) * (resist_slope * dose))
            for k in range(kernels):
                a, b, c, e = fields(at, piece, k)
                a, b, c, e = a * slopes[0], b * slopes[0], c * slopes[1], e * slopes[1]
                for base, where, value in ((0, 0, a + c), (0, side, b + e), (half, 0, b - e), (half, side, c - a)):
                    high, low = split(value)
                    lanes = slice(where + k * cols, where + (k + 1) * cols)
                    dfield[0, pl.ds(base + at, piece), lanes] = high
                    dfield[1, pl.ds(base + at, piece), lanes] = low

    both = trans[...].reshape(2 * freq_count, 2 * half)

    @pl.loop(0, 2 * side // width)
    def _(i):
        lanes = pl.ds(pl.multiple_of(i * width, width), width)
        t = mm(both, dfield[0, :, lanes])
        dband[:, lanes] = t[:freq_count] + t[freq_count:] + mm(trans[0], dfield[1, :, lanes])

    pieces = []
    for k in range(kernels):
        one = jnp.concatenate([dband[:, k * cols : (k + 1) * cols], dband[:, side + k * cols : side + (k + 1) * cols]], 1)
        pieces.append(one * (2.0 * kernel_weights[0, k]))
    loads[4].wait()
    t = mm3(split(jnp.concatenate(pieces, 0)), (back_t[0], back_t[1]))
    z_re = jnp.zeros((freq_count, ring), f32)
    z_im = jnp.zeros((freq_count, ring), f32)
    for k in range(kernels):
        d_re = t[k * freq_count : (k + 1) * freq_count, :ring]
        d_im = t[k * freq_count : (k + 1) * freq_count, ring:]
        g_re, g_im = gains[k, :, :ring], gains[k, :, ring:]
        z_re = z_re + (g_re * d_re + g_im * d_im)
        z_im = z_im + (g_re * d_im - g_im * d_re)
    t = mm3(split(jnp.concatenate([z_re, z_im], 0)), (direct[0], direct[1]))
    dspec = jnp.concatenate(
        [t[:freq_count, :ring] - t[freq_count:, ring:], t[:freq_count, ring:] + t[freq_count:, :ring]], 0
    )
    fold = ein.shape[2]
    groups = share // fold
    lane = lax.broadcasted_iota(jnp.int32, (fold, cols), 1)
    for n in range(nodes):
        dparts[n] = dspec[n * share : (n + 1) * share, cols:]
        for side_id in range(2):
            packed = None
            for g in range(groups):
                block = dspec[n * share + g * fold : n * share + (g + 1) * fold, :cols]
                if g == 0:
                    packed = block
                    continue
                moved = pltpu.roll(block, g * radius if side_id == 0 else cols - g * radius, 1)
                there = lane >= g * radius if side_id == 0 else lane < cols - g * radius
                packed = jnp.where(there, moved, packed)
            dedges[side_id, n] = packed

    def z_copy(d):
        return pltpu.make_async_remote_copy(
            src_ref=dparts.at[after(d)], dst_ref=zin.at[d], send_sem=z_send.at[d],
            recv_sem=z_recv.at[d], device_id=(tile, after(d)), device_id_type=MESH,
        )

    def e_copy(d, side_id):
        to = right if side_id == 0 else left
        return pltpu.make_async_remote_copy(
            src_ref=dedges.at[side_id, after(d)], dst_ref=ein.at[side_id, d], send_sem=e_send.at[side_id, d],
            recv_sem=e_recv.at[side_id, d], device_id=(to, after(d)), device_id_type=MESH,
        )

    copies = []
    for d in range(nodes):
        copies += [e_copy(d, 0), e_copy(d, 1)]
        if d:
            copies.append(z_copy(d))
    for copy in copies:
        copy.start()
    for copy in copies:
        copy.wait()
    value = dparts[node]
    from_left, from_right = ein[0, 0], ein[1, 0]
    for d in range(1, nodes):
        value = value + zin[d]
        from_left, from_right = from_left + ein[0, d], from_right + ein[1, d]
    keep_left = jnp.where((lane < radius) & (tile > 0), 1.0, 0.0)
    keep_right = jnp.where((lane >= cols - radius) & (tile < tiles - 1), 1.0, 0.0)
    edges = []
    for g in range(groups):
        a, b = from_left, from_right
        if g:
            a, b = pltpu.roll(a, cols - g * radius, 1), pltpu.roll(b, g * radius, 1)
        edges.append(a * keep_left + b * keep_right)
    value = value + jnp.concatenate(edges, 0)
    total[...] = value
    gathered[node] = value

    def g_copy(d):
        return pltpu.make_async_remote_copy(
            src_ref=total, dst_ref=gathered.at[node], send_sem=g_send.at[d],
            recv_sem=g_recv.at[d], device_id=(tile, after(d)), device_id_type=MESH,
        )

    for d in range(1, nodes):
        g_copy(d).start()
    for d in range(1, nodes):
        g_copy(d).wait()
    summed = jnp.concatenate([gathered[n] for n in range(nodes)], 0)
    out[...] = mm3((own_table[0], own_table[1]), split(summed))


def local(
    tiles, nodes,
    mask_field, kernel_taps, kernel_weights, node_weights, node_index, freq_index, chaos_weights, target,
):
    rows, cols = mask_field.shape
    _, kernels, _, freq_count, tap_count = kernel_taps.shape
    radius = (tap_count - 1) // 2
    half, chunk = rows // 2, rows // 2 // nodes
    terms = chaos_weights.shape[0]
    ring = 2 * cols
    share = 2 * freq_count // nodes
    piece = min(32, chunk)
    fold = 8 if share % 8 == 0 and share // 8 * radius <= cols else share
    direct, back, back_t = column_tables(cols, radius, freq_count)
    vmem = pl.BlockSpec(memory_space=pltpu.VMEM)
    hbm = pl.BlockSpec(memory_space=pl.ANY)
    smem = pltpu.SMEM
    scratch = pltpu.VMEM
    dma = pltpu.SemaphoreType.DMA
    return pl.pallas_call(
        functools.partial(kernel, tiles, nodes, radius),
        out_shape=jax.ShapeDtypeStruct((rows // nodes, cols), f32),
        in_specs=[hbm] * 11,
        out_specs=vmem,
        scratch_shapes=[
            smem(kernel_weights.shape, f32),
            smem(node_weights.shape, f32),
            smem(node_index.shape[::-1], jnp.int32),
            smem(freq_index.shape, jnp.int32),
            smem(chaos_weights.shape, f32),
            scratch((rows, cols), f32),
            scratch((2 * kernels, freq_count, tap_count), f32),
            scratch(direct.shape, bf16),
            scratch(back.shape, bf16),
            scratch(back_t.shape, bf16),
            scratch((freq_count, 128), jnp.int32),
            scratch((8, 256), jnp.int32),
            scratch((rows, 3 * freq_count), bf16),
            smem((nodes, terms), f32),
            scratch((2, freq_count, 2 * half), bf16),
            scratch((2, rows // nodes, 2 * freq_count), bf16),
            scratch((2 * kernels * freq_count, 128), f32),
            scratch((kernels, freq_count, 2 * ring), f32),
            scratch((2 * freq_count, cols), f32),
            scratch((2, 2 * freq_count, cols), f32),
            scratch((3 * freq_count, 2 * kernels * cols), bf16),
            scratch((rows, 2 * kernels * cols), f32),
            scratch((2, half, cols), f32),
            scratch((nodes, chunk // piece, 2, piece, cols), bf16),
            scratch((nodes, chunk // piece, 2, piece, cols), bf16),
            scratch((2, terms, chunk, cols), bf16),
            scratch((nodes, chunk // piece, 2, piece, cols), bf16),
            scratch((nodes, chunk // piece, 2, piece, cols), bf16),
            scratch((chunk // piece, 2, piece, cols), f32),
            scratch((2, piece, cols), f32),
            scratch((2, 2 * half, 2 * kernels * cols), bf16),
            scratch((freq_count, 2 * kernels * cols), f32),
            scratch((nodes, share, cols), f32),
            scratch((2, nodes, fold, cols), f32),
            scratch((nodes, share, cols), f32),
            scratch((2, nodes, fold, cols), f32),
            scratch((share, cols), f32),
            scratch((nodes, share, cols), f32),
            dma((12,)), dma((2,)), dma((2,)),
            dma((nodes, chunk // piece)), dma((nodes, chunk // piece)), dma((nodes, chunk // piece)), dma((nodes, chunk // piece)),
            dma((nodes,)), dma((nodes,)), dma((2, nodes)), dma((2, nodes)),
            dma((nodes,)), dma((nodes,)),
        ],
        compiler_params=pltpu.CompilerParams(
            collective_id=0, has_side_effects=True, vmem_limit_bytes=63 * 1024 * 1024
        ),
        name="mask_gradient",
    )(
        mask_field, kernel_taps.reshape(2 * kernels, freq_count, tap_count), kernel_weights, node_weights,
        node_index.T, freq_index, chaos_weights, target, direct, back, back_t,
    )


def solution(mesh):
    placed = (
        P(None, "tile"),
        P("node", None, None, None, None),
        P("node", None),
        P(),
        P(),
        P(),
        P(),
        P(None, None, "tile"),
    )
    return jax.shard_map(
        functools.partial(local, mesh.shape["tile"], mesh.shape["node"]),
        mesh=mesh, in_specs=placed, out_specs=P("node", "tile"), check_vma=False,
    )
```

```python
import functools
import math

import jax
import jax.numpy as jnp
import ml_dtypes
import numpy as np
from jax import lax
from jax.experimental import pallas as pl
from jax.experimental.pallas import tpu as pltpu
from jax.sharding import PartitionSpec as P

LEVELS = 5
DEGREES = 5
MESH = pl.DeviceIdType.MESH
bf16 = jnp.bfloat16
f32 = jnp.float32
resist_slope = 4.0
resist_level = 0.6


def split(value):
    high = value.astype(bf16)
    return high, (value - high.astype(f32)).astype(bf16)


def mm(left, right):
    return jnp.dot(left, right, preferred_element_type=f32)


def mm3(left, right):
    count = left[0].shape[0]
    both = mm(jnp.concatenate(left, 0), right[0])
    return both[:count] + (mm(left[0], right[1]) + both[count:])


def half_turn_cosine(step, half):
    folded = jnp.abs((step & (2 * half - 1)) - half).astype(f32)
    t = folded * (2.0 / half) - 1.0
    s = t * t
    acc = jnp.full_like(t, 5.6921729e-8)
    for c in (-3.5988432e-6, 1.6044118e-4, -4.6817541e-3, 7.9692626e-2, -0.64596410, 1.57079633):
        acc = acc * s + c
    return acc * t


def encode(value):
    scaled = value * 2.0**20
    square = scaled * scaled
    fourth = square * square
    return jnp.where(value < 0.0, -fourth, fourth).astype(bf16)


def decode(code):
    code = code.astype(f32)
    size = jnp.sqrt(jnp.sqrt(jnp.abs(code))) * 2.0**-20
    return jnp.where(code < 0.0, -size, size)


def legendre(u):
    s = u * u
    return [None, u, 1.5 * s - 0.5, (2.5 * s - 1.5) * u, (4.375 * s - 3.75) * s + 0.375]


def level(index):
    return index.astype(f32) * (2.0 / (LEVELS - 1)) - 1.0


def basis_of(node_index, node):
    focus = legendre(level(node_index[0, node]))
    dose = legendre(level(node_index[1, node]))
    terms = []
    for degree in range(DEGREES):
        for p in range(degree, -1, -1):
            a, b = focus[p], dose[degree - p]
            terms.append(1.0 if a is None and b is None else b if a is None else a if b is None else a * b)
    return terms


def column_tables(cols, radius, freq_count):
    ring = 2 * cols
    w = np.arange(ring)
    angle = 2 * np.pi * ((w[:, None] * w[None, :]) % ring) / ring
    direct = np.concatenate([np.cos(angle), np.sin(angle)], 1)
    out = 2 * np.pi * ((w[:, None] * (np.arange(cols) + cols - radius)[None, :]) % ring) / ring
    c, s = np.cos(out), np.sin(out)
    back = np.concatenate([np.concatenate([c, s], 1), np.concatenate([-s, c], 1)], 0)
    back = back / (ring * math.sqrt(freq_count))
    pieces = []
    for table in (direct, back, back.T):
        high = table.astype(ml_dtypes.bfloat16)
        low = (table - high.astype(np.float64)).astype(ml_dtypes.bfloat16)
        pieces.append(np.stack([high, low]))
    return pieces


def kernel(
    tiles, nodes, radius,
    mask_hbm, taps_hbm, kernel_weights_hbm, node_weights_hbm, node_index_hbm, freq_hbm, chaos_weights_hbm, target,
    direct_hbm, back_hbm, back_t_hbm,
    out,
    kernel_weights, node_weights, node_index, freq, chaos_weights,
    mask, taps, direct, back, back_t,
    freq_rows, freq_lanes, row_table, scaled, trans, own_table, padded_taps, gains,
    own_spec, halo, stacked, parts_of, resist, own_image, images, term,
    push, pressure, own_pressure, dfield, dparts, dedges, zin, ein, total, gathered,
    local_sem, halo_send, halo_recv, image_send, image_recv, push_send, push_recv,
    z_send, z_recv, e_send, e_recv, g_send, g_recv,
):
    tile, node = lax.axis_index("tile"), lax.axis_index("node")
    right, left = lax.rem(tile + 1, tiles), lax.rem(tile + tiles - 1, tiles)
    rows, cols = mask.shape
    half = rows // 2
    chunk = half // nodes
    freq_count = freq.shape[0]
    terms = chaos_weights.shape[0]
    kernels = taps.shape[0] // 2
    share = 2 * freq_count // nodes

    def after(d):
        return lax.rem(node + d, nodes)

    def before(d):
        return lax.rem(node + nodes - d, nodes)

    barrier = pltpu.get_barrier_semaphore()
    for d in range(1, nodes):
        pl.semaphore_signal(barrier, inc=1, device_id=(tile, after(d)), device_id_type=MESH)
    for d in range(nodes):
        pl.semaphore_signal(barrier, inc=1, device_id=(right, after(d)), device_id_type=MESH)
        pl.semaphore_signal(barrier, inc=1, device_id=(left, after(d)), device_id_type=MESH)

    loads = []
    for i, (source, held) in enumerate((
        (mask_hbm, mask), (direct_hbm, direct), (taps_hbm, taps), (back_hbm, back), (back_t_hbm, back_t),
        (kernel_weights_hbm, kernel_weights), (node_weights_hbm, node_weights),
        (node_index_hbm, node_index), (freq_hbm, freq), (chaos_weights_hbm, chaos_weights),
    )):
        loads.append(pltpu.make_async_copy(source, held, local_sem.at[i + 2]))
    for load in [loads[8]] + loads[:3] + loads[5:8] + loads[9:]:
        load.start()
    upper = pltpu.make_async_copy(
        target.at[:, pl.ds(pl.multiple_of(node * chunk, chunk), chunk), :], term.at[0], local_sem.at[0]
    )
    lower = pltpu.make_async_copy(
        target.at[:, pl.ds(pl.multiple_of(rows - (node + 1) * chunk, chunk), chunk), :],
        term.at[1], local_sem.at[1],
    )
    upper.start()
    lower.start()
    for load in loads[3:5]:
        load.start()

    loads[8].wait()
    row_id = lax.broadcasted_iota(jnp.int32, freq_rows.shape, 0)
    lane_id = lax.broadcasted_iota(jnp.int32, freq_lanes.shape, 1) % freq_count
    by_row = jnp.zeros(freq_rows.shape, jnp.int32)
    by_lane = jnp.zeros(freq_lanes.shape, jnp.int32)
    for i in range(freq_count):
        by_row = jnp.where(row_id == i, freq[i], by_row)
        by_lane = jnp.where(lane_id == i, freq[i], by_lane)
    freq_rows[...] = by_row
    freq_lanes[...] = by_lane

    place = lax.broadcasted_iota(jnp.int32, (freq_count, half), 1)
    step = freq_rows[:, :1] * (2 * place + 1)
    c_high, c_low = split(half_turn_cosine(step, rows))
    s_high, s_low = split(half_turn_cosine(step - half, rows))
    trans[0, :, :half] = c_high
    trans[1, :, :half] = c_low
    trans[0, :, half:] = s_high
    trans[1, :, half:] = s_low

    ri = lax.broadcasted_iota(jnp.int32, (half, half), 0)
    ci = lax.broadcasted_iota(jnp.int32, (half, half), 1)
    mirror = jnp.where(ri + ci == half - 1, 1.0, 0.0).astype(bf16)
    loads[0].wait()
    m_high, m_low = split(mask[half:, :])
    mirrored = mm(mirror, m_high) + mm(mirror, m_low)
    top = mask[:half, :]
    norm = 1.0 / math.sqrt(rows)
    own_spec[:freq_count, :] = mm3((c_high, c_low), split(top + mirrored)) * norm
    own_spec[freq_count:, :] = mm3((s_high, s_low), split(top - mirrored)) * -norm

    pl.semaphore_wait(barrier, 3 * nodes - 1)
    halo_copies = []
    for side, to in ((0, right), (1, left)):
        halo_copies.append(pltpu.make_async_remote_copy(
            src_ref=own_spec, dst_ref=halo.at[side], send_sem=halo_send.at[side],
            recv_sem=halo_recv.at[side], device_id=(to, node), device_id_type=MESH,
        ))
        halo_copies[-1].start()

    wide = 3 * freq_count
    place = lax.broadcasted_iota(jnp.int32, (half, wide), 0)
    lane = lax.broadcasted_iota(jnp.int32, (half, wide), 1)
    middle = (lane >= freq_count) & (lane < 2 * freq_count)
    step = freq_lanes[:1, :wide] * (2 * place + 1)
    for first_row, shift in ((0, 0), (half, half)):
        value = half_turn_cosine(step - shift, rows)
        rounded = value.astype(bf16).astype(f32)
        row_table[first_row : first_row + half, :] = jnp.where(middle, value - rounded, rounded).astype(bf16)

    for load in loads[5:8] + loads[9:]:
        load.wait()
    for d in range(nodes):
        n = before(d)
        for j, b in enumerate(basis_of(node_index, n)):
            scaled[d, j] = node_weights[n] * b

    own_rows = rows // nodes
    place = lax.broadcasted_iota(jnp.int32, (own_rows, 2 * freq_count), 0) + node * own_rows
    lane = lax.broadcasted_iota(jnp.int32, (own_rows, 2 * freq_count), 1)
    step = freq_lanes[:1, : 2 * freq_count] * (2 * place + 1)
    step = jnp.where(lane < freq_count, step, step + half)
    own_table[0], own_table[1] = split(half_turn_cosine(step, rows) * norm)

    padded_taps[...] = jnp.zeros(padded_taps.shape, f32)
    loads[1].wait()
    loads[2].wait()
    for i in range(2 * kernels):
        padded_taps[i * freq_count : (i + 1) * freq_count, : 2 * radius + 1] = taps[i]
    near = padded_taps.shape[1]
    ring = 2 * cols
    t = mm3(split(padded_taps[...]), (direct[0, :near, :], direct[1, :near, :]))
    for k in range(kernels):
        re = t[2 * k * freq_count : (2 * k + 1) * freq_count]
        im = t[(2 * k + 1) * freq_count : (2 * k + 2) * freq_count]
        gains[k, :, :ring] = re[:, :ring] - im[:, ring:]
        gains[k, :, ring:] = re[:, ring:] + im[:, :ring]

    ri = lax.broadcasted_iota(jnp.int32, (chunk, chunk), 0)
    ci = lax.broadcasted_iota(jnp.int32, (chunk, chunk), 1)
    small_mirror = jnp.where(ri + ci == chunk - 1, 1.0, 0.0).astype(bf16)
    upper.wait()
    lower.wait()
    turned = mm(small_mirror, jnp.concatenate([term[1, j] for j in range(terms)], 1)).astype(bf16)
    for j in range(terms):
        term[1, j] = turned[:, j * cols : (j + 1) * cols]

    for copy in halo_copies:
        copy.wait()
    lane = lax.broadcasted_iota(jnp.int32, (2 * freq_count, cols), 1)
    keep_left = jnp.where((lane >= cols - radius) & (tile > 0), 1.0, 0.0)
    keep_right = jnp.where((lane < radius) & (tile < tiles - 1), 1.0, 0.0)
    around = jnp.concatenate([halo[0] * keep_left + halo[1] * keep_right, own_spec[...]], 1)
    t = mm3(split(around), (direct[0], direct[1]))
    a_re = t[:freq_count, :ring] + t[freq_count:, ring:]
    a_im = t[freq_count:, :ring] - t[:freq_count, ring:]
    products = []
    for k in range(kernels):
        g_re, g_im = gains[k, :, :ring], gains[k, :, ring:]
        products.append(jnp.concatenate([a_re * g_re - a_im * g_im, a_re * g_im + a_im * g_re], 1))
    loads[3].wait()
    band = mm3(split(jnp.concatenate(products, 0)), (back[0], back[1]))
    for k in range(kernels):
        high, low = split(band[k * freq_count : (k + 1) * freq_count])
        for part in range(2):
            at = (part * kernels + k) * cols
            source = slice(part * cols, (part + 1) * cols)
            stacked[:freq_count, at : at + cols] = high[:, source]
            stacked[freq_count : 2 * freq_count, at : at + cols] = high[:, source]
            stacked[2 * freq_count :, at : at + cols] = low[:, source]

    def image_copy(d, part):
        return pltpu.make_async_remote_copy(
            src_ref=own_image.at[after(d), part], dst_ref=images.at[d, part], send_sem=image_send.at[d, part],
            recv_sem=image_recv.at[d, part], device_id=(tile, after(d)), device_id_type=MESH,
        )

    dose = 1.0 + 0.1 * level(node_index[1, node])
    side = kernels * cols
    parts_of[...] = mm(row_table[...], stacked[...])

    def fields(row, count, k):
        p = parts_of[pl.ds(row, count), k * cols : (k + 1) * cols]
        t = parts_of[pl.ds(row, count), side + k * cols : side + (k + 1) * cols]
        r = parts_of[pl.ds(half + row, count), k * cols : (k + 1) * cols]
        q = parts_of[pl.ds(half + row, count), side + k * cols : side + (k + 1) * cols]
        return p - q, r + t, p + q, t - r

    piece = images.shape[3]
    parts = chunk // piece

    @pl.loop(0, parts)
    def _(part):
        for d in list(range(1, nodes)) + [0]:
            mine = after(d)
            at = pl.multiple_of(mine * chunk + part * piece, piece)
            first = jnp.zeros((piece, cols), f32)
            second = jnp.zeros((piece, cols), f32)
            for k in range(kernels):
                a, b, c, e = fields(at, piece, k)
                weight = kernel_weights[0, k]
                first = first + weight * (a * a + b * b)
                second = second + weight * (c * c + e * e)
            for h, intensity in ((0, first), (1, second)):
                value = jax.nn.sigmoid(resist_slope * (dose * intensity - resist_level))
                resist[h, pl.ds(at, piece), :] = value
                own_image[mine, part, h] = value.astype(bf16)
            if d:
                image_copy(d, part).start()

    images[0] = own_image[node]

    def push_copy(d, part):
        return pltpu.make_async_remote_copy(
            src_ref=push.at[d, part], dst_ref=pressure.at[d, part], send_sem=push_send.at[d, part],
            recv_sem=push_recv.at[d, part], device_id=(tile, before(d)), device_id_type=MESH,
        )

    @pl.loop(0, parts)
    def _(part):
        for d in range(1, nodes):
            image_copy(d, part).wait()

        @pl.loop(0, 2)
        def _(h):
            seen = [images[d, part, h].astype(f32) for d in range(nodes)]
            sums = [None] * nodes
            for j in range(terms):
                coefficient = scaled[0, j] * seen[0]
                for d in range(1, nodes):
                    coefficient = coefficient + scaled[d, j] * seen[d]
                wanted = term[h, j, pl.ds(pl.multiple_of(part * piece, piece), piece), :]
                mixed = chaos_weights[j] * jnp.tanh(coefficient - wanted.astype(f32))
                for d in range(nodes):
                    one = scaled[d, j] * mixed
                    sums[d] = one if sums[d] is None else sums[d] + one
            for d in range(nodes):
                if d:
                    push[d, part, h] = encode(sums[d])
                else:
                    own_pressure[part, h] = sums[d]

        for d in range(1, nodes):
            push_copy(d, part).start()

    @pl.loop(0, parts)
    def _(part):
        def back_one(d, given):
            at = pl.multiple_of(after(d) * chunk + part * piece, piece)
            slopes = []
            for h in range(2):
                value = resist[h, pl.ds(at, piece), :]
                slopes.append(given[h] * value * (1.0 - value) * (resist_slope * dose))
            for k in range(kernels):
                a, b, c, e = fields(at, piece, k)
                a, b, c, e = a * slopes[0], b * slopes[0], c * slopes[1], e * slopes[1]
                for base, where, value in ((0, 0, a + c), (0, side, b + e), (half, 0, b - e), (half, side, c - a)):
                    high, low = split(value)
                    lanes = slice(where + k * cols, where + (k + 1) * cols)
                    dfield[0, pl.ds(base + at, piece), lanes] = high
                    dfield[1, pl.ds(base + at, piece), lanes] = low

        back_one(0, own_pressure[part])
        for d in range(1, nodes):
            push_copy(d, part).wait()
        for d in range(1, nodes):
            back_one(d, decode(pressure[d, part]))

    both = trans[...].reshape(2 * freq_count, 2 * half)

    t = mm(both, dfield[0])
    dband = t[:freq_count] + t[freq_count:] + mm(trans[0], dfield[1])
    pieces = []
    for k in range(kernels):
        one = jnp.concatenate([dband[:, k * cols : (k + 1) * cols], dband[:, side + k * cols : side + (k + 1) * cols]], 1)
        pieces.append(one * (2.0 * kernel_weights[0, k]))
    loads[4].wait()
    t = mm3(split(jnp.concatenate(pieces, 0)), (back_t[0], back_t[1]))
    z_re = jnp.zeros((freq_count, ring), f32)
    z_im = jnp.zeros((freq_count, ring), f32)
    for k in range(kernels):
        d_re = t[k * freq_count : (k + 1) * freq_count, :ring]
        d_im = t[k * freq_count : (k + 1) * freq_count, ring:]
        g_re, g_im = gains[k, :, :ring], gains[k, :, ring:]
        z_re = z_re + (g_re * d_re + g_im * d_im)
        z_im = z_im + (g_re * d_im - g_im * d_re)
    t = mm3(split(jnp.concatenate([z_re, z_im], 0)), (direct[0], direct[1]))
    dspec = jnp.concatenate(
        [t[:freq_count, :ring] - t[freq_count:, ring:], t[:freq_count, ring:] + t[freq_count:, :ring]], 0
    )
    fold = ein.shape[2]
    groups = share // fold
    lane = lax.broadcasted_iota(jnp.int32, (fold, cols), 1)
    for n in range(nodes):
        dparts[n] = dspec[n * share : (n + 1) * share, cols:]
        for side_id in range(2):
            packed = None
            for g in range(groups):
                block = dspec[n * share + g * fold : n * share + (g + 1) * fold, :cols]
                if g == 0:
                    packed = block
                    continue
                moved = pltpu.roll(block, g * radius if side_id == 0 else cols - g * radius, 1)
                there = lane >= g * radius if side_id == 0 else lane < cols - g * radius
                packed = jnp.where(there, moved, packed)
            dedges[side_id, n] = packed

    def z_copy(d):
        return pltpu.make_async_remote_copy(
            src_ref=dparts.at[after(d)], dst_ref=zin.at[d], send_sem=z_send.at[d],
            recv_sem=z_recv.at[d], device_id=(tile, after(d)), device_id_type=MESH,
        )

    def e_copy(d, side_id):
        to = right if side_id == 0 else left
        return pltpu.make_async_remote_copy(
            src_ref=dedges.at[side_id, after(d)], dst_ref=ein.at[side_id, d], send_sem=e_send.at[side_id, d],
            recv_sem=e_recv.at[side_id, d], device_id=(to, after(d)), device_id_type=MESH,
        )

    copies = []
    for d in range(nodes):
        copies += [e_copy(d, 0), e_copy(d, 1)]
        if d:
            copies.append(z_copy(d))
    for copy in copies:
        copy.start()
    for copy in copies:
        copy.wait()
    value = dparts[node]
    from_left, from_right = ein[0, 0], ein[1, 0]
    for d in range(1, nodes):
        value = value + zin[d]
        from_left, from_right = from_left + ein[0, d], from_right + ein[1, d]
    keep_left = jnp.where((lane < radius) & (tile > 0), 1.0, 0.0)
    keep_right = jnp.where((lane >= cols - radius) & (tile < tiles - 1), 1.0, 0.0)
    edges = []
    for g in range(groups):
        a, b = from_left, from_right
        if g:
            a, b = pltpu.roll(a, cols - g * radius, 1), pltpu.roll(b, g * radius, 1)
        edges.append(a * keep_left + b * keep_right)
    value = value + jnp.concatenate(edges, 0)
    total[...] = value
    gathered[node] = value

    def g_copy(d):
        return pltpu.make_async_remote_copy(
            src_ref=total, dst_ref=gathered.at[node], send_sem=g_send.at[d],
            recv_sem=g_recv.at[d], device_id=(tile, after(d)), device_id_type=MESH,
        )

    for d in range(1, nodes):
        g_copy(d).start()
    for d in range(1, nodes):
        g_copy(d).wait()
    summed = jnp.concatenate([gathered[n] for n in range(nodes)], 0)
    out[...] = mm3((own_table[0], own_table[1]), split(summed))


def local(
    tiles, nodes,
    mask_field, kernel_taps, kernel_weights, node_weights, node_index, freq_index, chaos_weights, target,
):
    rows, cols = mask_field.shape
    _, kernels, _, freq_count, tap_count = kernel_taps.shape
    radius = (tap_count - 1) // 2
    half, chunk = rows // 2, rows // 2 // nodes
    terms = chaos_weights.shape[0]
    ring = 2 * cols
    share = 2 * freq_count // nodes
    piece = min(32, chunk)
    fold = 8 if share % 8 == 0 and share // 8 * radius <= cols else share
    direct, back, back_t = column_tables(cols, radius, freq_count)
    vmem = pl.BlockSpec(memory_space=pltpu.VMEM)
    hbm = pl.BlockSpec(memory_space=pl.ANY)
    smem = pltpu.SMEM
    scratch = pltpu.VMEM
    dma = pltpu.SemaphoreType.DMA
    return pl.pallas_call(
        functools.partial(kernel, tiles, nodes, radius),
        out_shape=jax.ShapeDtypeStruct((rows // nodes, cols), f32),
        in_specs=[hbm] * 11,
        out_specs=vmem,
        scratch_shapes=[
            smem(kernel_weights.shape, f32),
            smem(node_weights.shape, f32),
            smem(node_index.shape[::-1], jnp.int32),
            smem(freq_index.shape, jnp.int32),
            smem(chaos_weights.shape, f32),
            scratch((rows, cols), f32),
            scratch((2 * kernels, freq_count, tap_count), f32),
            scratch(direct.shape, bf16),
            scratch(back.shape, bf16),
            scratch(back_t.shape, bf16),
            scratch((freq_count, 128), jnp.int32),
            scratch((8, 256), jnp.int32),
            scratch((rows, 3 * freq_count), bf16),
            smem((nodes, terms), f32),
            scratch((2, freq_count, 2 * half), bf16),
            scratch((2, rows // nodes, 2 * freq_count), bf16),
            scratch((2 * kernels * freq_count, 128), f32),
            scratch((kernels, freq_count, 2 * ring), f32),
            scratch((2 * freq_count, cols), f32),
            scratch((2, 2 * freq_count, cols), f32),
            scratch((3 * freq_count, 2 * kernels * cols), bf16),
            scratch((rows, 2 * kernels * cols), f32),
            scratch((2, half, cols), f32),
            scratch((nodes, chunk // piece, 2, piece, cols), bf16),
            scratch((nodes, chunk // piece, 2, piece, cols), bf16),
            scratch((2, terms, chunk, cols), bf16),
            scratch((nodes, chunk // piece, 2, piece, cols), bf16),
            scratch((nodes, chunk // piece, 2, piece, cols), bf16),
            scratch((chunk // piece, 2, piece, cols), f32),
            scratch((2, 2 * half, 2 * kernels * cols), bf16),
            scratch((nodes, share, cols), f32),
            scratch((2, nodes, fold, cols), f32),
            scratch((nodes, share, cols), f32),
            scratch((2, nodes, fold, cols), f32),
            scratch((share, cols), f32),
            scratch((nodes, share, cols), f32),
            dma((12,)), dma((2,)), dma((2,)),
            dma((nodes, chunk // piece)), dma((nodes, chunk // piece)), dma((nodes, chunk // piece)), dma((nodes, chunk // piece)),
            dma((nodes,)), dma((nodes,)), dma((2, nodes)), dma((2, nodes)),
            dma((nodes,)), dma((nodes,)),
        ],
        compiler_params=pltpu.CompilerParams(
            collective_id=0, has_side_effects=True, vmem_limit_bytes=63 * 1024 * 1024
        ),
        name="mask_gradient",
    )(
        mask_field, kernel_taps.reshape(2 * kernels, freq_count, tap_count), kernel_weights, node_weights,
        node_index.T, freq_index, chaos_weights, target, direct, back, back_t,
    )


def solution(mesh):
    placed = (
        P(None, "tile"),
        P("node", None, None, None, None),
        P("node", None),
        P(),
        P(),
        P(),
        P(),
        P(None, None, "tile"),
    )
    return jax.shard_map(
        functools.partial(local, mesh.shape["tile"], mesh.shape["node"]),
        mesh=mesh, in_specs=placed, out_specs=P("node", "tile"), check_vma=False,
    )
```

```python
import functools
import math

import jax
import jax.numpy as jnp
import ml_dtypes
import numpy as np
from jax import lax
from jax.experimental import pallas as pl
from jax.experimental.pallas import tpu as pltpu
from jax.sharding import PartitionSpec as P

LEVELS = 5
DEGREES = 5
MESH = pl.DeviceIdType.MESH
bf16 = jnp.bfloat16
f32 = jnp.float32
resist_slope = 4.0
resist_level = 0.6


def split(value):
    high = value.astype(bf16)
    return high, (value - high.astype(f32)).astype(bf16)


def mm(left, right):
    return jnp.dot(left, right, preferred_element_type=f32)


def mm3(left, right):
    count = left[0].shape[0]
    both = mm(jnp.concatenate(left, 0), right[0])
    return both[:count] + (mm(left[0], right[1]) + both[count:])


def half_turn_cosine(step, half):
    folded = jnp.abs((step & (2 * half - 1)) - half).astype(f32)
    t = folded * (2.0 / half) - 1.0
    s = t * t
    acc = jnp.full_like(t, 5.6921729e-8)
    for c in (-3.5988432e-6, 1.6044118e-4, -4.6817541e-3, 7.9692626e-2, -0.64596410, 1.57079633):
        acc = acc * s + c
    return acc * t


def encode(value):
    scaled = value * 2.0**20
    square = scaled * scaled
    fourth = square * square
    return jnp.where(value < 0.0, -fourth, fourth).astype(bf16)


def decode(code):
    code = code.astype(f32)
    size = jnp.sqrt(jnp.sqrt(jnp.abs(code))) * 2.0**-20
    return jnp.where(code < 0.0, -size, size)


def legendre(u):
    s = u * u
    return [None, u, 1.5 * s - 0.5, (2.5 * s - 1.5) * u, (4.375 * s - 3.75) * s + 0.375]


def level(index):
    return index.astype(f32) * (2.0 / (LEVELS - 1)) - 1.0


def basis_of(node_index, node):
    focus = legendre(level(node_index[0, node]))
    dose = legendre(level(node_index[1, node]))
    terms = []
    for degree in range(DEGREES):
        for p in range(degree, -1, -1):
            a, b = focus[p], dose[degree - p]
            terms.append(1.0 if a is None and b is None else b if a is None else a if b is None else a * b)
    return terms


def column_tables(cols, radius, freq_count):
    ring = 2 * cols
    w = np.arange(ring)
    angle = 2 * np.pi * ((w[:, None] * w[None, :]) % ring) / ring
    direct = np.concatenate([np.cos(angle), np.sin(angle)], 1)
    out = 2 * np.pi * ((w[:, None] * (np.arange(cols) + cols - radius)[None, :]) % ring) / ring
    c, s = np.cos(out), np.sin(out)
    back = np.concatenate([np.concatenate([c, s], 1), np.concatenate([-s, c], 1)], 0)
    back = back / (ring * math.sqrt(freq_count))
    pieces = []
    for table in (direct, back, back.T):
        high = table.astype(ml_dtypes.bfloat16)
        low = (table - high.astype(np.float64)).astype(ml_dtypes.bfloat16)
        pieces.append(np.stack([high, low]))
    return pieces


def kernel(
    tiles, nodes, radius,
    mask_hbm, taps_hbm, kernel_weights_hbm, node_weights_hbm, node_index_hbm, freq_hbm, chaos_weights_hbm, target,
    direct_hbm, back_hbm, back_t_hbm,
    out,
    kernel_weights, node_weights, node_index, freq, chaos_weights,
    mask, taps, direct, back, back_t,
    freq_rows, freq_lanes, row_table, scaled, trans, own_table, padded_taps, gains,
    own_spec, halo, stacked, parts_of, resist, own_image, images, term,
    push, pressure, own_pressure, dfield, dparts, dedges, zin, ein, total, gathered,
    local_sem, halo_send, halo_recv, image_send, image_recv, push_send, push_recv,
    z_send, z_recv, e_send, e_recv, g_send, g_recv,
):
    tile, node = lax.axis_index("tile"), lax.axis_index("node")
    right, left = lax.rem(tile + 1, tiles), lax.rem(tile + tiles - 1, tiles)
    rows, cols = mask.shape
    half = rows // 2
    chunk = half // nodes
    freq_count = freq.shape[0]
    terms = chaos_weights.shape[0]
    kernels = taps.shape[0] // 2
    share = 2 * freq_count // nodes

    def after(d):
        return lax.rem(node + d, nodes)

    def before(d):
        return lax.rem(node + nodes - d, nodes)

    barrier = pltpu.get_barrier_semaphore()
    for d in range(1, nodes):
        pl.semaphore_signal(barrier, inc=1, device_id=(tile, after(d)), device_id_type=MESH)
    for d in range(nodes):
        pl.semaphore_signal(barrier, inc=1, device_id=(right, after(d)), device_id_type=MESH)
        pl.semaphore_signal(barrier, inc=1, device_id=(left, after(d)), device_id_type=MESH)

    loads = []
    for i, (source, held) in enumerate((
        (mask_hbm, mask), (direct_hbm, direct), (taps_hbm, taps), (back_hbm, back), (back_t_hbm, back_t),
        (kernel_weights_hbm, kernel_weights), (node_weights_hbm, node_weights),
        (node_index_hbm, node_index), (freq_hbm, freq), (chaos_weights_hbm, chaos_weights),
    )):
        loads.append(pltpu.make_async_copy(source, held, local_sem.at[i + 2]))
    for load in [loads[8]] + loads[:3] + loads[5:8] + loads[9:]:
        load.start()
    upper = pltpu.make_async_copy(
        target.at[:, pl.ds(pl.multiple_of(node * chunk, chunk), chunk), :], term.at[0], local_sem.at[0]
    )
    lower = pltpu.make_async_copy(
        target.at[:, pl.ds(pl.multiple_of(rows - (node + 1) * chunk, chunk), chunk), :],
        term.at[1], local_sem.at[1],
    )
    upper.start()
    lower.start()
    for load in loads[3:5]:
        load.start()

    loads[8].wait()
    row_id = lax.broadcasted_iota(jnp.int32, freq_rows.shape, 0)
    lane_id = lax.broadcasted_iota(jnp.int32, freq_lanes.shape, 1) % freq_count
    by_row = jnp.zeros(freq_rows.shape, jnp.int32)
    by_lane = jnp.zeros(freq_lanes.shape, jnp.int32)
    for i in range(freq_count):
        by_row = jnp.where(row_id == i, freq[i], by_row)
        by_lane = jnp.where(lane_id == i, freq[i], by_lane)
    freq_rows[...] = by_row
    freq_lanes[...] = by_lane

    place = lax.broadcasted_iota(jnp.int32, (freq_count, half), 1)
    step = freq_rows[:, :1] * (2 * place + 1)
    c_high, c_low = split(half_turn_cosine(step, rows))
    s_high, s_low = split(half_turn_cosine(step - half, rows))
    trans[0, :, :half] = c_high
    trans[1, :, :half] = c_low
    trans[0, :, half:] = s_high
    trans[1, :, half:] = s_low

    ri = lax.broadcasted_iota(jnp.int32, (half, half), 0)
    ci = lax.broadcasted_iota(jnp.int32, (half, half), 1)
    mirror = jnp.where(ri + ci == half - 1, 1.0, 0.0).astype(bf16)
    loads[0].wait()
    m_high, m_low = split(mask[half:, :])
    mirrored = mm(mirror, m_high) + mm(mirror, m_low)
    top = mask[:half, :]
    norm = 1.0 / math.sqrt(rows)
    own_spec[:freq_count, :] = mm3((c_high, c_low), split(top + mirrored)) * norm
    own_spec[freq_count:, :] = mm3((s_high, s_low), split(top - mirrored)) * -norm

    pl.semaphore_wait(barrier, 3 * nodes - 1)
    halo_copies = []
    for side, to in ((0, right), (1, left)):
        halo_copies.append(pltpu.make_async_remote_copy(
            src_ref=own_spec, dst_ref=halo.at[side], send_sem=halo_send.at[side],
            recv_sem=halo_recv.at[side], device_id=(to, node), device_id_type=MESH,
        ))
        halo_copies[-1].start()

    wide = 3 * freq_count
    place = lax.broadcasted_iota(jnp.int32, (half, wide), 0)
    lane = lax.broadcasted_iota(jnp.int32, (half, wide), 1)
    middle = (lane >= freq_count) & (lane < 2 * freq_count)
    step = freq_lanes[:1, :wide] * (2 * place + 1)
    for first_row, shift in ((0, 0), (half, half)):
        value = half_turn_cosine(step - shift, rows)
        rounded = value.astype(bf16).astype(f32)
        row_table[first_row : first_row + half, :] = jnp.where(middle, value - rounded, rounded).astype(bf16)

    for load in loads[5:8] + loads[9:]:
        load.wait()
    padded_taps[...] = jnp.zeros(padded_taps.shape, f32)
    loads[1].wait()
    loads[2].wait()
    for i in range(2 * kernels):
        padded_taps[i * freq_count : (i + 1) * freq_count, : 2 * radius + 1] = taps[i]
    near = padded_taps.shape[1]
    ring = 2 * cols
    t = mm3(split(padded_taps[...]), (direct[0, :near, :], direct[1, :near, :]))
    for k in range(kernels):
        re = t[2 * k * freq_count : (2 * k + 1) * freq_count]
        im = t[(2 * k + 1) * freq_count : (2 * k + 2) * freq_count]
        gains[k, :, :ring] = re[:, :ring] - im[:, ring:]
        gains[k, :, ring:] = re[:, ring:] + im[:, :ring]

    for copy in halo_copies:
        copy.wait()
    lane = lax.broadcasted_iota(jnp.int32, (2 * freq_count, cols), 1)
    keep_left = jnp.where((lane >= cols - radius) & (tile > 0), 1.0, 0.0)
    keep_right = jnp.where((lane < radius) & (tile < tiles - 1), 1.0, 0.0)
    around = jnp.concatenate([halo[0] * keep_left + halo[1] * keep_right, own_spec[...]], 1)
    t = mm3(split(around), (direct[0], direct[1]))
    a_re = t[:freq_count, :ring] + t[freq_count:, ring:]
    a_im = t[freq_count:, :ring] - t[:freq_count, ring:]
    products = []
    for k in range(kernels):
        g_re, g_im = gains[k, :, :ring], gains[k, :, ring:]
        products.append(jnp.concatenate([a_re * g_re - a_im * g_im, a_re * g_im + a_im * g_re], 1))
    loads[3].wait()
    band = mm3(split(jnp.concatenate(products, 0)), (back[0], back[1]))
    for k in range(kernels):
        high, low = split(band[k * freq_count : (k + 1) * freq_count])
        for part in range(2):
            at = (part * kernels + k) * cols
            source = slice(part * cols, (part + 1) * cols)
            stacked[:freq_count, at : at + cols] = high[:, source]
            stacked[freq_count : 2 * freq_count, at : at + cols] = high[:, source]
            stacked[2 * freq_count :, at : at + cols] = low[:, source]

    def image_copy(d, part):
        return pltpu.make_async_remote_copy(
            src_ref=own_image.at[after(d), part], dst_ref=images.at[d, part], send_sem=image_send.at[d, part],
            recv_sem=image_recv.at[d, part], device_id=(tile, after(d)), device_id_type=MESH,
        )

    dose = 1.0 + 0.1 * level(node_index[1, node])
    side = kernels * cols
    parts_of[...] = mm(row_table[...], stacked[...])

    def fields(row, count, k):
        p = parts_of[pl.ds(row, count), k * cols : (k + 1) * cols]
        t = parts_of[pl.ds(row, count), side + k * cols : side + (k + 1) * cols]
        r = parts_of[pl.ds(half + row, count), k * cols : (k + 1) * cols]
        q = parts_of[pl.ds(half + row, count), side + k * cols : side + (k + 1) * cols]
        return p - q, r + t, p + q, t - r

    piece = images.shape[3]
    parts = chunk // piece

    @pl.loop(0, parts)
    def _(part):
        for d in list(range(1, nodes)) + [0]:
            mine = after(d)
            at = pl.multiple_of(mine * chunk + part * piece, piece)
            first = jnp.zeros((piece, cols), f32)
            second = jnp.zeros((piece, cols), f32)
            for k in range(kernels):
                a, b, c, e = fields(at, piece, k)
                weight = kernel_weights[0, k]
                first = first + weight * (a * a + b * b)
                second = second + weight * (c * c + e * e)
            for h, intensity in ((0, first), (1, second)):
                value = jax.nn.sigmoid(resist_slope * (dose * intensity - resist_level))
                resist[h, pl.ds(at, piece), :] = value
                own_image[mine, part, h] = value.astype(bf16)
            if d:
                image_copy(d, part).start()

    images[0] = own_image[node]

    for d in range(nodes):
        n = before(d)
        for j, b in enumerate(basis_of(node_index, n)):
            scaled[d, j] = node_weights[n] * b

    ri = lax.broadcasted_iota(jnp.int32, (chunk, chunk), 0)
    ci = lax.broadcasted_iota(jnp.int32, (chunk, chunk), 1)
    small_mirror = jnp.where(ri + ci == chunk - 1, 1.0, 0.0).astype(bf16)
    upper.wait()
    lower.wait()
    turned = mm(small_mirror, jnp.concatenate([term[1, j] for j in range(terms)], 1)).astype(bf16)
    for j in range(terms):
        term[1, j] = turned[:, j * cols : (j + 1) * cols]

    def push_copy(d, part):
        return pltpu.make_async_remote_copy(
            src_ref=push.at[d, part], dst_ref=pressure.at[d, part], send_sem=push_send.at[d, part],
            recv_sem=push_recv.at[d, part], device_id=(tile, before(d)), device_id_type=MESH,
        )

    @pl.loop(0, parts)
    def _(part):
        for d in range(1, nodes):
            image_copy(d, part).wait()

        @pl.loop(0, 2)
        def _(h):
            seen = [images[d, part, h].astype(f32) for d in range(nodes)]
            sums = [None] * nodes
            for j in range(terms):
                coefficient = scaled[0, j] * seen[0]
                for d in range(1, nodes):
                    coefficient = coefficient + scaled[d, j] * seen[d]
                wanted = term[h, j, pl.ds(pl.multiple_of(part * piece, piece), piece), :]
                mixed = chaos_weights[j] * jnp.tanh(coefficient - wanted.astype(f32))
                for d in range(nodes):
                    one = scaled[d, j] * mixed
                    sums[d] = one if sums[d] is None else sums[d] + one
            for d in range(nodes):
                if d:
                    push[d, part, h] = encode(sums[d])
                else:
                    own_pressure[part, h] = sums[d]

        for d in range(1, nodes):
            push_copy(d, part).start()

    own_rows = rows // nodes
    place = lax.broadcasted_iota(jnp.int32, (own_rows, 2 * freq_count), 0) + node * own_rows
    lane = lax.broadcasted_iota(jnp.int32, (own_rows, 2 * freq_count), 1)
    step = freq_lanes[:1, : 2 * freq_count] * (2 * place + 1)
    step = jnp.where(lane < freq_count, step, step + half)
    own_table[0], own_table[1] = split(half_turn_cosine(step, rows) * norm)

    @pl.loop(0, parts)
    def _(part):
        def back_one(d, given):
            at = pl.multiple_of(after(d) * chunk + part * piece, piece)
            slopes = []
            for h in range(2):
                value = resist[h, pl.ds(at, piece), :]
                slopes.append(given[h] * value * (1.0 - value) * (resist_slope * dose))
            for k in range(kernels):
                a, b, c, e = fields(at, piece, k)
                a, b, c, e = a * slopes[0], b * slopes[0], c * slopes[1], e * slopes[1]
                for base, where, value in ((0, 0, a + c), (0, side, b + e), (half, 0, b - e), (half, side, c - a)):
                    high, low = split(value)
                    lanes = slice(where + k * cols, where + (k + 1) * cols)
                    dfield[0, pl.ds(base + at, piece), lanes] = high
                    dfield[1, pl.ds(base + at, piece), lanes] = low

        back_one(0, own_pressure[part])
        for d in range(1, nodes):
            push_copy(d, part).wait()
        for d in range(1, nodes):
            back_one(d, decode(pressure[d, part]))

    both = trans[...].reshape(2 * freq_count, 2 * half)

    t = mm(both, dfield[0])
    dband = t[:freq_count] + t[freq_count:] + mm(trans[0], dfield[1])
    pieces = []
    for k in range(kernels):
        one = jnp.concatenate([dband[:, k * cols : (k + 1) * cols], dband[:, side + k * cols : side + (k + 1) * cols]], 1)
        pieces.append(one * (2.0 * kernel_weights[0, k]))
    loads[4].wait()
    t = mm3(split(jnp.concatenate(pieces, 0)), (back_t[0], back_t[1]))
    z_re = jnp.zeros((freq_count, ring), f32)
    z_im = jnp.zeros((freq_count, ring), f32)
    for k in range(kernels):
        d_re = t[k * freq_count : (k + 1) * freq_count, :ring]
        d_im = t[k * freq_count : (k + 1) * freq_count, ring:]
        g_re, g_im = gains[k, :, :ring], gains[k, :, ring:]
        z_re = z_re + (g_re * d_re + g_im * d_im)
        z_im = z_im + (g_re * d_im - g_im * d_re)
    t = mm3(split(jnp.concatenate([z_re, z_im], 0)), (direct[0], direct[1]))
    dspec = jnp.concatenate(
        [t[:freq_count, :ring] - t[freq_count:, ring:], t[:freq_count, ring:] + t[freq_count:, :ring]], 0
    )
    fold = ein.shape[2]
    groups = share // fold
    lane = lax.broadcasted_iota(jnp.int32, (fold, cols), 1)
    for n in range(nodes):
        dparts[n] = dspec[n * share : (n + 1) * share, cols:]
        for side_id in range(2):
            packed = None
            for g in range(groups):
                block = dspec[n * share + g * fold : n * share + (g + 1) * fold, :cols]
                if g == 0:
                    packed = block
                    continue
                moved = pltpu.roll(block, g * radius if side_id == 0 else cols - g * radius, 1)
                there = lane >= g * radius if side_id == 0 else lane < cols - g * radius
                packed = jnp.where(there, moved, packed)
            dedges[side_id, n] = packed

    def z_copy(d):
        return pltpu.make_async_remote_copy(
            src_ref=dparts.at[after(d)], dst_ref=zin.at[d], send_sem=z_send.at[d],
            recv_sem=z_recv.at[d], device_id=(tile, after(d)), device_id_type=MESH,
        )

    def e_copy(d, side_id):
        to = right if side_id == 0 else left
        return pltpu.make_async_remote_copy(
            src_ref=dedges.at[side_id, after(d)], dst_ref=ein.at[side_id, d], send_sem=e_send.at[side_id, d],
            recv_sem=e_recv.at[side_id, d], device_id=(to, after(d)), device_id_type=MESH,
        )

    copies = []
    for d in range(nodes):
        copies += [e_copy(d, 0), e_copy(d, 1)]
        if d:
            copies.append(z_copy(d))
    for copy in copies:
        copy.start()
    for copy in copies:
        copy.wait()
    value = dparts[node]
    from_left, from_right = ein[0, 0], ein[1, 0]
    for d in range(1, nodes):
        value = value + zin[d]
        from_left, from_right = from_left + ein[0, d], from_right + ein[1, d]
    keep_left = jnp.where((lane < radius) & (tile > 0), 1.0, 0.0)
    keep_right = jnp.where((lane >= cols - radius) & (tile < tiles - 1), 1.0, 0.0)
    edges = []
    for g in range(groups):
        a, b = from_left, from_right
        if g:
            a, b = pltpu.roll(a, cols - g * radius, 1), pltpu.roll(b, g * radius, 1)
        edges.append(a * keep_left + b * keep_right)
    value = value + jnp.concatenate(edges, 0)
    total[...] = value
    gathered[node] = value

    def g_copy(d):
        return pltpu.make_async_remote_copy(
            src_ref=total, dst_ref=gathered.at[node], send_sem=g_send.at[d],
            recv_sem=g_recv.at[d], device_id=(tile, after(d)), device_id_type=MESH,
        )

    for d in range(1, nodes):
        g_copy(d).start()
    for d in range(1, nodes):
        g_copy(d).wait()
    summed = jnp.concatenate([gathered[n] for n in range(nodes)], 0)
    out[...] = mm3((own_table[0], own_table[1]), split(summed))


def local(
    tiles, nodes,
    mask_field, kernel_taps, kernel_weights, node_weights, node_index, freq_index, chaos_weights, target,
):
    rows, cols = mask_field.shape
    _, kernels, _, freq_count, tap_count = kernel_taps.shape
    radius = (tap_count - 1) // 2
    half, chunk = rows // 2, rows // 2 // nodes
    terms = chaos_weights.shape[0]
    ring = 2 * cols
    share = 2 * freq_count // nodes
    piece = min(32, chunk)
    fold = 8 if share % 8 == 0 and share // 8 * radius <= cols else share
    direct, back, back_t = column_tables(cols, radius, freq_count)
    vmem = pl.BlockSpec(memory_space=pltpu.VMEM)
    hbm = pl.BlockSpec(memory_space=pl.ANY)
    smem = pltpu.SMEM
    scratch = pltpu.VMEM
    dma = pltpu.SemaphoreType.DMA
    return pl.pallas_call(
        functools.partial(kernel, tiles, nodes, radius),
        out_shape=jax.ShapeDtypeStruct((rows // nodes, cols), f32),
        in_specs=[hbm] * 11,
        out_specs=vmem,
        scratch_shapes=[
            smem(kernel_weights.shape, f32),
            smem(node_weights.shape, f32),
            smem(node_index.shape[::-1], jnp.int32),
            smem(freq_index.shape, jnp.int32),
            smem(chaos_weights.shape, f32),
            scratch((rows, cols), f32),
            scratch((2 * kernels, freq_count, tap_count), f32),
            scratch(direct.shape, bf16),
            scratch(back.shape, bf16),
            scratch(back_t.shape, bf16),
            scratch((freq_count, 128), jnp.int32),
            scratch((8, 256), jnp.int32),
            scratch((rows, 3 * freq_count), bf16),
            smem((nodes, terms), f32),
            scratch((2, freq_count, 2 * half), bf16),
            scratch((2, rows // nodes, 2 * freq_count), bf16),
            scratch((2 * kernels * freq_count, 128), f32),
            scratch((kernels, freq_count, 2 * ring), f32),
            scratch((2 * freq_count, cols), f32),
            scratch((2, 2 * freq_count, cols), f32),
            scratch((3 * freq_count, 2 * kernels * cols), bf16),
            scratch((rows, 2 * kernels * cols), f32),
            scratch((2, half, cols), f32),
            scratch((nodes, chunk // piece, 2, piece, cols), bf16),
            scratch((nodes, chunk // piece, 2, piece, cols), bf16),
            scratch((2, terms, chunk, cols), bf16),
            scratch((nodes, chunk // piece, 2, piece, cols), bf16),
            scratch((nodes, chunk // piece, 2, piece, cols), bf16),
            scratch((chunk // piece, 2, piece, cols), f32),
            scratch((2, 2 * half, 2 * kernels * cols), bf16),
            scratch((nodes, share, cols), f32),
            scratch((2, nodes, fold, cols), f32),
            scratch((nodes, share, cols), f32),
            scratch((2, nodes, fold, cols), f32),
            scratch((share, cols), f32),
            scratch((nodes, share, cols), f32),
            dma((12,)), dma((2,)), dma((2,)),
            dma((nodes, chunk // piece)), dma((nodes, chunk // piece)), dma((nodes, chunk // piece)), dma((nodes, chunk // piece)),
            dma((nodes,)), dma((nodes,)), dma((2, nodes)), dma((2, nodes)),
            dma((nodes,)), dma((nodes,)),
        ],
        compiler_params=pltpu.CompilerParams(
            collective_id=0, has_side_effects=True, vmem_limit_bytes=63 * 1024 * 1024
        ),
        name="mask_gradient",
    )(
        mask_field, kernel_taps.reshape(2 * kernels, freq_count, tap_count), kernel_weights, node_weights,
        node_index.T, freq_index, chaos_weights, target, direct, back, back_t,
    )


def solution(mesh):
    placed = (
        P(None, "tile"),
        P("node", None, None, None, None),
        P("node", None),
        P(),
        P(),
        P(),
        P(),
        P(None, None, "tile"),
    )
    return jax.shard_map(
        functools.partial(local, mesh.shape["tile"], mesh.shape["node"]),
        mesh=mesh, in_specs=placed, out_specs=P("node", "tile"), check_vma=False,
    )
```
